128 devices in a mesh: dp: 32 (over x, z, core), tensor: 4 (over y).
Axes of the slice: x: 4, y: 4, z: 4, core: 2. Of those that a mesh axis runs over, the one named last changes fastest.
Arguments:
- activations: bfloat16 [3072, 8192], P('dp', 'tensor'), may hold values from -6.5 to 6.5
- targets: bfloat16 [3072, 8192], P('dp', 'tensor'), may hold values from -22 to 22
- key_weight: bfloat16 [8192, 1024], P('dp', 'tensor'), may hold values from -6 to 6
Outputs:
- rotated: float32 [8192, 1024], P('dp', 'tensor')
The draws below stay inside these ranges and needn't reach their ends.
All inputs are finite; a program needn't handle non-finite values.
Results may differ from the reference program's by a relative error of at most 0.0003.
Values may be sent and summed in bfloat16 or wider, within the bound.
A program may use at most 64 MiB of HBM per device.

```python
import math
import jax
import jax.numpy as jnp
from jax import lax

D = 8192
F = 1024
ITERS = 2
TOKENS = 3072


def shared_values(key):
    return jnp.clip(jax.random.normal(key, (TOKENS, D), jnp.float32), -6.0, 6.0)


def draw_activations(key, part):
    common = shared_values(key)
    values = common
    return values.astype(jnp.bfloat16)


def draw_targets(key, part):
    common = shared_values(key)
    key = jax.random.fold_in(key, 23)
    noise_key, scale_key = jax.random.split(key)
    own_noise = jnp.clip(jax.random.normal(noise_key, (TOKENS, D), jnp.float32), -6.0, 6.0)
    row_ramp = 0.6 + 1.2 * jnp.arange(TOKENS, dtype=jnp.float32)[:, None] / (TOKENS - 1)
    jitter = jnp.exp(jax.random.uniform(scale_key, (TOKENS, 1), jnp.float32, minval=math.log(0.7), maxval=math.log(1.4)))
    values = (0.6 * common + 0.8 * own_noise) * row_ramp * jitter
    return values.astype(jnp.bfloat16)


def shard_levels(rng, shape, cuts, smallest, top_value):
    factor_of = 1.0
    for position, blocks in cuts:
        heights = jax.random.uniform(jax.random.fold_in(jax.random.fold_in(rng, 6), position), (blocks,), jnp.float32, smallest / len(cuts), top_value / len(cuts))
        factor_of = factor_of * jnp.repeat(jnp.exp(heights), shape[position] // blocks).reshape((-1,) + (1,) * (len(shape) - 1 - position))
    return factor_of


def gaussian(stream_key, shape, width, most, shards=(), kind=jnp.bfloat16):
    drawn = width * jax.random.normal(stream_key, shape, jnp.float32)
    if shards:
        drawn = drawn * shard_levels(stream_key, shape, shards, -0.22, 0.18)
    return jnp.clip(drawn, -most, most).astype(kind)


def setup_inputs(seed: int = 0) -> dict:
    seeds = jax.random.split(jax.random.key(seed), 4)
    return {
        "activations": draw_activations(jax.random.fold_in(seeds[3], 71), 0),
        "targets": draw_targets(jax.random.fold_in(seeds[3], 71), 0),
        "key_weight": gaussian(seeds[2], (D, F), 1.0, 6.0, ((0, 32), (1, 4))),
    }


ridge_weight = 0.5


def reference(activations, targets, key_weight):
    token_count = activations.shape[0]
    kernel = lax.dot_general(activations, activations, (((1,), (1,)), ((), ())), preferred_element_type=jnp.float32) / token_count
    rhs = jnp.dot(targets, key_weight, preferred_element_type=jnp.float32)
    dual_state = jnp.zeros_like(rhs)
    residual = rhs
    direction = rhs
    resid_norm = jnp.sum(residual * residual, axis=0)
    for step_index in range(ITERS):
        image = jnp.dot(kernel, direction, precision=lax.Precision.HIGHEST) + ridge_weight * direction
        step_alpha = resid_norm / jnp.sum(direction * image, axis=0)
        dual_state = dual_state + step_alpha * direction
        residual = residual - step_alpha * image
        new_norm = jnp.sum(residual * residual, axis=0)
        direction = residual + (new_norm / resid_norm) * direction
        resid_norm = new_norm
    rotated = lax.dot_general(activations.astype(jnp.float32), dual_state, (((0,), (0,)), ((), ())), precision=lax.Precision.HIGHEST) / token_count
    return rotated
```

```python
import jax
import jax.numpy as jnp
from jax import lax
from jax.experimental import pallas as pl
from jax.experimental.pallas import tpu as pltpu
from jax.sharding import PartitionSpec as P

MESH = pl.DeviceIdType.MESH
TOKENS = 3072
RIDGE = 0.5
F32, BF16 = jnp.float32, jnp.bfloat16


def device(x, y, z, c):
    return (x * 8 + z * 2 + c, y)


def split(value):
    high = value.astype(BF16)
    return high, (value - high.astype(F32)).astype(BF16)


class Copies:
    def __init__(self, send, recv):
        self.send, self.recv, self.started = send, recv, []

    def start(self, index, src, dst, target):
        copy = pltpu.make_async_remote_copy(
            src_ref=src,
            dst_ref=dst,
            send_sem=self.send.at[index],
            recv_sem=self.recv.at[index],
            device_id=target,
            device_id_type=MESH,
        )
        copy.start()
        self.started.append(copy)

    def arrived(self, index, dst, source):
        pltpu.make_async_remote_copy(
            src_ref=dst,
            dst_ref=dst,
            send_sem=self.send.at[index],
            recv_sem=self.recv.at[index],
            device_id=source,
            device_id_type=MESH,
        ).wait_recv()

    def finish(self):
        for copy in self.started:
            copy.wait_send()


def kernel(
    x_ref, y_ref, w_ref, out_ref,
    y_sort, y_all, w_all, x_mine, x_all, x_full, x_flip,
    b_part, b_other, b_all, b_pair, u0, u_pair, ud,
    v_part, v_in1, v_sum, v_in2, v_all, r_all, gamma, o_mine, o_in,
    y_s, y_r, w_s, w_r, x_s, x_r, xy_s, xy_r, xc_s, xc_r, p_s, p_r,
    b_s, b_r, v_s, v_r, g_s, g_r, o_s, o_r,
):
    i = lax.axis_index("dp")
    y = lax.axis_index("tensor")
    x, z, c = i // 8, lax.rem(i // 2, 4), lax.rem(i, 2)
    mine = x * 4 + z
    twin = 1 - c

    def at(a, d):
        return lax.rem(a + d, 4)

    barrier = pltpu.get_barrier_semaphore()
    partners = [(dx, dz) for dx in range(4) for dz in range(4) if dx or dz]
    peers = [device(at(x, dx), y, at(z, dz), c) for dx, dz in partners]
    peers += [device(x, at(y, d), z, e) for d in range(1, 4) for e in (c, twin)]
    peers += [device(x, y, z, twin)]
    slot = lax.rem(z, 2) * 2 + c
    owner = z // 2
    stays = jnp.logical_and(x == z, owner == c)
    for k in range(4):

        @pl.when(jnp.logical_not(jnp.logical_and(stays, slot == k)))
        def _():
            pl.semaphore_signal(barrier, inc=1, device_id=device(z, y, 2 * c + k // 2, k % 2), device_id_type=MESH)

    for peer in peers:
        pl.semaphore_signal(barrier, inc=1, device_id=peer, device_id_type=MESH)

    for e in range(2):
        for h in range(2):
            for q in range(4):
                y_sort[e, :, h * 512 + q * 128 : h * 512 + q * 128 + 128] = y_ref[
                    :, q * 512 + e * 256 + h * 128 : q * 512 + e * 256 + h * 128 + 128
                ]
    for h in range(2):
        w_all[h, mine] = w_ref[h * 128 : h * 128 + 128, :]
    pl.semaphore_wait(barrier, len(peers) + 4 - stays.astype(jnp.int32))

    wc = Copies(w_s, w_r)
    yc = Copies(y_s, y_r)
    xc = Copies(x_s, x_r)
    bc = Copies(b_s, b_r)
    vc = Copies(v_s, v_r)

    def gather_first(copies, buf):
        for d in range(1, 4):
            copies.start(d - 1, buf.at[0, mine], buf.at[0, mine], device(at(x, d), y, z, c))
            copies.start(d + 2, buf.at[1, mine], buf.at[1, mine], device(x, y, at(z, d), c))

    def forward(copies, buf, j):
        block0 = at(x, 4 - j) * 4 + z
        block1 = x * 4 + at(z, 4 - j)
        if j:
            copies.arrived(j - 1, buf.at[0, block0], device(at(x, 4 - j), y, z, c))
        for d in range(1, 4):
            copies.start(6 + j * 3 + d - 1, buf.at[0, block0], buf.at[0, block0], device(x, y, at(z, d), c))
        if j:
            copies.arrived(j + 2, buf.at[1, block1], device(x, y, at(z, 4 - j), c))
        for d in range(1, 4):
            copies.start(18 + j * 3 + d - 1, buf.at[1, block1], buf.at[1, block1], device(at(x, d), y, z, c))

    def gather_last(copies, buf):
        for j in range(4):
            for d in range(1, 4):
                block0 = at(x, 4 - j) * 4 + at(z, 4 - d)
                copies.arrived(6 + j * 3 + d - 1, buf.at[0, block0], device(x, y, at(z, 4 - d), c))
                block1 = at(x, 4 - d) * 4 + at(z, 4 - j)
                copies.arrived(18 + j * 3 + d - 1, buf.at[1, block1], device(at(x, 4 - d), y, z, c))

    gather_first(wc, w_all)
    for d in range(4):
        for e in range(2):
            if d or e:
                target = lax.rem(c + e, 2)
                yc.start(d * 2 + e, y_sort.at[target], y_all.at[y, c], device(x, at(y, d), z, target))
    y_all[y, c] = y_sort[c]
    for k, (dx, dz) in enumerate(partners):
        block = at(x, dx) * 4 + at(z, dz)
        columns = pl.ds(pl.multiple_of(block * 128, 128), 128)
        xc.start(k, x_ref.at[:, columns], x_mine.at[mine], device(at(x, dx), y, at(z, dz), c))
    x_mine[mine] = x_ref[:, pl.ds(pl.multiple_of(mine * 128, 128), 128)]

    for j in (0, 1, 3, 2):
        forward(wc, w_all, j)
    for k, (dx, dz) in enumerate(partners):
        sx, sz = at(x, 4 - dx), at(z, 4 - dz)
        xc.arrived(k, x_mine.at[sx * 4 + sz], device(sx, y, sz, c))
    for d in range(4):
        for e in range(2):
            if d or e:
                source = lax.rem(c + e, 2)
                yc.arrived(d * 2 + e, y_all.at[at(y, 4 - d), source], device(x, at(y, 4 - d), z, source))

    xyc = Copies(xy_s, xy_r)
    xcc = Copies(xc_s, xc_r)
    for d in range(1, 4):
        xyc.start(d - 1, x_mine, x_all.at[y, c], device(x, at(y, d), z, c))
    xcc.start(0, x_mine, x_all.at[y, c], device(x, y, z, twin))
    x_all[y, c] = x_mine[...]
    gather_last(wc, w_all)

    part = jnp.zeros((192, 256), F32)
    for s in range(4):
        for h in range(2):
            part += jnp.dot(
                y_all[s, :, :, h * 512 : h * 512 + 512].reshape(192, 512),
                w_all[h, 4 * s : 4 * s + 4].reshape(512, 256),
                preferred_element_type=F32,
            )
    b_part[0] = part[:, :128]
    b_part[1] = part[:, 128:]
    pc = Copies(p_s, p_r)
    pc.start(0, b_part.at[twin], b_other, device(x, y, z, twin))
    pc.arrived(0, b_other, device(x, y, z, twin))
    for h in range(2):
        b_all[h, mine] = b_part[c, h * 96 : h * 96 + 96] + b_other[h * 96 : h * 96 + 96]
    gather_first(bc, b_all)
    for j in (0, 1, 3, 2):
        forward(bc, b_all, j)

    for d in range(1, 4):
        source = at(y, 4 - d)
        xyc.arrived(d - 1, x_all.at[source, c], device(x, source, z, c))
        xcc.start(d, x_all.at[source, c], x_all.at[source, c], device(x, y, z, twin))
    for d in range(4):
        source = at(y, 4 - d)
        xcc.arrived(d, x_all.at[source, twin], device(x, y, z, twin))

    for s in range(4):
        for e in range(2):
            piece = x_all[s, e].reshape(1536, 128)
            x_full[e * 1536 : e * 1536 + 1536, s * 128 : s * 128 + 128] = piece
            x_flip[s * 128 : s * 128 + 128, e * 1536 : e * 1536 + 1536] = piece.T

    gather_last(bc, b_all)
    bb = jnp.zeros((1, 128), F32)
    for h in range(2):
        value = b_all[h].reshape(1536, 128)
        bb += jnp.sum(value * value, axis=0, keepdims=True)
        high, low = split(value)
        b_pair[h * 1536 : h * 1536 + 1536, :128] = high
        b_pair[h * 1536 : h * 1536 + 1536, 128:] = low
    wide = jnp.dot(x_flip[...], b_pair[...], preferred_element_type=F32)
    first = wide[:, :128] + wide[:, 128:]
    u0[...] = first
    high, low = split(first * (1.0 / TOKENS))
    u_pair[:, :128] = high
    u_pair[:, 128:] = low

    def block_of(h, place):
        rows = pl.ds(pl.multiple_of(h * 1536 + place * 384, 128), 384)
        wide = jnp.dot(x_full[rows, :], u_pair[...], preferred_element_type=F32)
        v_part[h, place] = (wide[:, :128] + wide[:, 128:]).reshape(4, 96, 128)

    for d in (1, 3, 2):
        block_of(0, at(x, d))
        vc.start(36 + d - 1, v_part.at[0, at(x, d)], v_in1.at[0, d - 1], device(at(x, d), y, z, c))
    for place in range(4):
        block_of(1, place)
    for d in (1, 3, 2):
        vc.start(39 + d - 1, v_part.at[1, :, at(z, d)], v_in1.at[1, d - 1], device(x, y, at(z, d), c))
    block_of(0, x)
    for d in (1, 3, 2):
        vc.arrived(36 + d - 1, v_in1.at[0, d - 1], device(at(x, 4 - d), y, z, c))
    v_sum[0] = v_part[0, x] + v_in1[0, 0] + v_in1[0, 1] + v_in1[0, 2]
    for d in (1, 3, 2):
        vc.start(30 + d - 1, v_sum.at[0, at(z, d)], v_in2.at[0, d - 1], device(x, y, at(z, d), c))
    for d in (1, 3, 2):
        vc.arrived(39 + d - 1, v_in1.at[1, d - 1], device(x, y, at(z, 4 - d), c))
    v_sum[1] = v_part[1, :, z] + v_in1[1, 0] + v_in1[1, 1] + v_in1[1, 2]
    for d in (1, 3, 2):
        vc.start(33 + d - 1, v_sum.at[1, at(x, d)], v_in2.at[1, d - 1], device(at(x, d), y, z, c))
    for d in (1, 3, 2):
        vc.arrived(30 + d - 1, v_in2.at[0, d - 1], device(x, y, at(z, 4 - d), c))
    v_all[0, mine] = v_sum[0, z] + v_in2[0, 0] + v_in2[0, 1] + v_in2[0, 2]
    for d in (1, 3, 2):
        vc.arrived(33 + d - 1, v_in2.at[1, d - 1], device(at(x, 4 - d), y, z, c))
    v_all[1, mine] = v_sum[1, x] + v_in2[1, 0] + v_in2[1, 1] + v_in2[1, 2]
    gather_first(vc, v_all)
    for j in (0, 1, 3, 2):
        forward(vc, v_all, j)
    gather_last(vc, v_all)

    bv = jnp.zeros((1, 128), F32)
    for h in range(2):
        bv += jnp.sum((b_all[h] * v_all[h]).reshape(1536, 128), axis=0, keepdims=True)
    alpha = bb / (bv + RIDGE * bb)
    norm = jnp.zeros((1, 128), F32)
    for h in range(2):
        value = b_all[h].reshape(1536, 128)
        residual = value - alpha * (v_all[h].reshape(1536, 128) + RIDGE * value)
        norm += jnp.sum(residual * residual, axis=0, keepdims=True)
        r_all[h] = residual
        high, low = split(residual)
        b_pair[h * 1536 : h * 1536 + 1536, :128] = high
        b_pair[h * 1536 : h * 1536 + 1536, 128:] = low
    beta = norm / bb
    wide = jnp.dot(x_flip[...], b_pair[...], preferred_element_type=F32)
    turned = wide[:, :128] + wide[:, 128:] + beta * u0[...]
    ud[...] = turned
    gamma[mine] = jnp.broadcast_to(jnp.sum(turned * turned, axis=0, keepdims=True), (8, 128))
    gc = Copies(g_s, g_r)
    for k, (dx, dz) in enumerate(partners):
        gc.start(k, gamma.at[mine], gamma.at[mine], device(at(x, dx), y, at(z, dz), c))
    dd = jnp.zeros((1, 128), F32)
    for h in range(2):
        turn = r_all[h] + beta * b_all[h].reshape(1536, 128)
        dd += jnp.sum(turn * turn, axis=0, keepdims=True)
    for k, (dx, dz) in enumerate(partners):
        sx, sz = at(x, 4 - dx), at(z, 4 - dz)
        gc.arrived(k, gamma.at[sx * 4 + sz], device(sx, y, sz, c))
    curve = jnp.sum(gamma[...], axis=0)[:1] * (1.0 / TOKENS) + RIDGE * dd
    step = norm / curve
    result = (alpha * u0[...] + step * ud[...]) * (1.0 / TOKENS)
    o_mine[...] = result.reshape(4, 128, 128)

    for p in range(4):
        place = at(x, p)

        def move(place=place):
            return pltpu.make_async_remote_copy(
                src_ref=o_mine.at[place], dst_ref=o_in.at[slot], send_sem=o_s.at[p], recv_sem=o_r.at[slot],
                device_id=device(place, y, x, owner), device_id_type=MESH,
            )

        if p:
            move().start()
        else:

            @pl.when(jnp.logical_not(stays))
            def _():
                move().start()

            @pl.when(stays)
            def _():
                pltpu.make_async_copy(o_mine.at[place], o_in.at[slot], o_r.at[slot]).start()

    for k in range(4):
        pltpu.make_async_copy(o_in.at[k], o_in.at[k], o_r.at[k]).wait()
        t, e = k // 2, k % 2
        out_ref[t * 128 : t * 128 + 128, e * 128 : e * 128 + 128] = o_in[k]
    for p in range(1, 4):
        pltpu.make_async_copy(o_mine.at[p], o_mine.at[p], o_s.at[p]).wait()

    @pl.when(jnp.logical_not(stays))
    def _():
        pltpu.make_async_copy(o_mine.at[0], o_mine.at[0], o_s.at[0]).wait()

    for copies in (wc, yc, xc, bc, vc, xyc, xcc, pc, gc):
        copies.finish()


def local(activations, targets, key_weight):
    vmem = pl.BlockSpec(memory_space=pltpu.VMEM)
    dma = pltpu.SemaphoreType.DMA
    sizes = (8, 30, 15, 3, 4, 1, 30, 42, 15, 4)
    buffers = [
        ((2, 96, 1024), BF16),
        ((4, 2, 96, 1024), BF16),
        ((2, 16, 128, 256), BF16),
        ((16, 96, 128), BF16),
        ((4, 2, 16, 96, 128), BF16),
        ((TOKENS, 512), BF16),
        ((512, TOKENS), BF16),
        ((2, 192, 128), F32),
        ((192, 128), F32),
        ((2, 16, 96, 128), F32),
        ((TOKENS, 256), BF16),
        ((512, 128), F32),
        ((512, 256), BF16),
        ((512, 128), F32),
        ((2, 4, 4, 96, 128), F32),
        ((2, 3, 4, 96, 128), F32),
        ((2, 4, 96, 128), F32),
        ((2, 3, 96, 128), F32),
        ((2, 16, 96, 128), F32),
        ((2, 1536, 128), F32),
        ((16, 8, 128), F32),
        ((4, 128, 128), F32),
        ((4, 128, 128), F32),
    ]
    return pl.pallas_call(
        kernel,
        out_shape=jax.ShapeDtypeStruct((256, 256), F32),
        in_specs=[vmem] * 3,
        out_specs=vmem,
        scratch_shapes=[pltpu.VMEM(*b) for b in buffers] + [dma((n,)) for n in sizes for _ in range(2)],
        compiler_params=pltpu.CompilerParams(collective_id=0, has_side_effects=True, vmem_limit_bytes=48 * 2**20),
    )(activations, targets, key_weight)


def solution(mesh):
    placed = (P("dp", "tensor"), P("dp", "tensor"), P("dp", "tensor"))
    return jax.shard_map(local, mesh=mesh, in_specs=placed, out_specs=P("dp", "tensor"), check_vma=False)
```

```python
import jax
import jax.numpy as jnp
from jax import lax
from jax.experimental import pallas as pl
from jax.experimental.pallas import tpu as pltpu
from jax.sharding import PartitionSpec as P

MESH = pl.DeviceIdType.MESH
TOKENS = 3072
RIDGE = 0.5
F32, BF16 = jnp.float32, jnp.bfloat16


def device(x, y, z, c):
    return (x * 8 + z * 2 + c, y)


def split(value):
    high = value.astype(BF16)
    return high, (value - high.astype(F32)).astype(BF16)


class Copies:
    def __init__(self, send, recv):
        self.send, self.recv, self.started = send, recv, []

    def start(self, index, src, dst, target, lands=None):
        copy = pltpu.make_async_remote_copy(
            src_ref=src,
            dst_ref=dst,
            send_sem=self.send.at[index],
            recv_sem=self.recv.at[index if lands is None else lands],
            device_id=target,
            device_id_type=MESH,
        )
        copy.start()
        self.started.append(copy)

    def arrived(self, index, dst):
        pltpu.make_async_copy(dst, dst, self.recv.at[index]).wait()

    def finish(self):
        for copy in self.started:
            copy.wait_send()


def kernel(
    x_in, y_in, w_in, out_ref,
    x_sort, y_sort, y_all, w_all, x_mine, x_all, x_full, x_flip,
    b_part, b_other, b_all, b_pair, u0, u_pair, ud,
    v_part, v_far, v_merge, v_near, v_sum, v_light, v_all, r_all, gamma, scalars, u_in, d_in,
    l_s, y_s, y_r, w_s, w_r, x_s, x_r, xy_s, xy_r, xc_s, xc_r, p_s, p_r,
    b_s, b_r, v_s, v_r, g_s, g_r, t_s, t_r, u_s, u_r, d_s, d_r,
):
    i = lax.axis_index("dp")
    y = lax.axis_index("tensor")
    x, z, c = i // 8, lax.rem(i // 2, 4), lax.rem(i, 2)
    mine = x * 4 + z
    twin = 1 - c

    def at(a, d):
        return lax.rem(a + d + 4, 4)

    partners = [(dx, dz) for dx in range(4) for dz in range(4) if dx or dz]
    up, down = at(y, 1), at(y, -1)

    slot = lax.rem(z, 2) * 2 + c
    owner = z // 2
    stays = jnp.logical_and(x == z, owner == c)
    barrier = pltpu.get_barrier_semaphore()
    peers = [device(at(x, dx), y, at(z, dz), c) for dx, dz in partners]
    peers += [device(x, place, z, e) for place in (up, down) for e in (c, twin)]
    peers += [device(x, y, z, twin)]
    for peer in peers:
        pl.semaphore_signal(barrier, inc=1, device_id=peer, device_id_type=MESH)
    for k in range(4):

        @pl.when(jnp.logical_not(jnp.logical_and(stays, slot == k)))
        def _():
            pl.semaphore_signal(barrier, inc=1, device_id=device(z, y, 2 * c + k // 2, k % 2), device_id_type=MESH)

    loads = []
    for h in range(2):
        loads.append((w_in.at[h * 128 : h * 128 + 128, :], w_all.at[h, mine]))
    for e in range(2):
        for h in range(2):
            for q in range(4):
                columns = slice(q * 512 + e * 256 + h * 128, q * 512 + e * 256 + h * 128 + 128)
                loads.append((y_in.at[:, columns], y_sort.at[e, :, h * 512 + q * 128 : h * 512 + q * 128 + 128]))
    for k in range(16):
        loads.append((x_in.at[:, k * 128 : k * 128 + 128], x_sort.at[k]))
    loads = [pltpu.make_async_copy(src, dst, l_s.at[k]) for k, (src, dst) in enumerate(loads)]
    for load in loads:
        load.start()
    for load in loads:
        load.wait()
    pl.semaphore_wait(barrier, len(peers) + 4 - stays.astype(jnp.int32))

    wc, yc, xc, xyc, xcc = Copies(w_s, w_r), Copies(y_s, y_r), Copies(x_s, x_r), Copies(xy_s, xy_r), Copies(xc_s, xc_r)
    pc, bc, vc = Copies(p_s, p_r), Copies(b_s, b_r), Copies(v_s, v_r)
    gc, tc, uc, dc = Copies(g_s, g_r), Copies(t_s, t_r), Copies(u_s, u_r), Copies(d_s, d_r)

    def light(h, d):
        return device(at(x, d), y, z, c) if h == 0 else device(x, y, at(z, d), c)

    def heavy(h, d):
        return device(x, y, at(z, d), c) if h == 0 else device(at(x, d), y, z, c)

    def block(h, dl, dh):
        return at(x, dl) * 4 + at(z, dh) if h == 0 else at(x, dh) * 4 + at(z, dl)

    def ring_first(copies, buf):
        for d in (1, 3, 2):
            for h in range(2):
                copies.start(h * 3 + d - 1, buf.at[h, mine], buf.at[h, mine], light(h, d))
        ring_heavy(copies, buf, 0)

    def ring_heavy(copies, buf, j):
        for h in range(2):
            part = buf.at[h, block(h, -j, 0)]
            if j:
                copies.arrived(h * 3 + j - 1, part)
            copies.start(6 + h * 8 + j * 2, part, part, heavy(h, 1))
            copies.start(6 + h * 8 + j * 2 + 1, part, part, heavy(h, -1))

    def ring_forward(copies, buf, j):
        for h in range(2):
            if j in (0, 1):
                part = buf.at[h, block(h, -j, -1)]
                copies.arrived(6 + h * 8 + j * 2, part)
                copies.start(22 + h * 4 + j, part, part, heavy(h, 1))
            else:
                part = buf.at[h, block(h, -j, 1)]
                copies.arrived(6 + h * 8 + j * 2 + 1, part)
                copies.start(22 + h * 4 + j, part, part, heavy(h, -1))

    def ring_last(copies, buf):
        for h in range(2):
            for j in (2, 3):
                copies.arrived(6 + h * 8 + j * 2, buf.at[h, block(h, -j, -1)])
            for j in (0, 1):
                copies.arrived(6 + h * 8 + j * 2 + 1, buf.at[h, block(h, -j, 1)])
            for j in range(4):
                copies.arrived(22 + h * 4 + j, buf.at[h, block(h, -j, 2)])

    def gather_first(copies, buf):
        for d in (1, 3, 2):
            for h in range(2):
                copies.start(h * 3 + d - 1, buf.at[h, mine], buf.at[h, mine], light(h, d))
        gather_heavy(copies, buf, 0)

    def gather_heavy(copies, buf, j):
        for h in range(2):
            part = buf.at[h, block(h, -j, 0)]
            if j:
                copies.arrived(h * 3 + j - 1, part)
            for d in (1, 3, 2):
                copies.start(6 + h * 12 + j * 3 + d - 1, part, part, heavy(h, d))

    def gather_last(copies, buf):
        for j in range(4):
            for h in range(2):
                for d in (1, 3, 2):
                    copies.arrived(6 + h * 12 + j * 3 + d - 1, buf.at[h, block(h, -j, -d)])

    ring_first(wc, w_all)
    for e in range(2):
        target = lax.rem(c + e, 2)
        yc.start(e, y_sort.at[target], y_all.at[y, c], device(x, up, z, target), lands=c)
        yc.start(2 + e, y_sort.at[target], y_all.at[y, c], device(x, down, z, target), lands=2 + c)
    yc.start(4, y_sort.at[twin], y_all.at[y, c], device(x, y, z, twin))
    for k, (dx, dz) in enumerate(partners):
        xc.start(k, x_sort.at[at(x, dx) * 4 + at(z, dz)], x_mine.at[mine], device(at(x, dx), y, at(z, dz), c))
    y_all[y, c] = y_sort[c]
    x_mine[mine] = x_sort[mine]

    for j in (1, 3, 2):
        ring_heavy(wc, w_all, j)
    ring_forward(wc, w_all, 0)
    ring_forward(wc, w_all, 1)
    yc.arrived(0, y_all.at[down, 0])
    yc.start(5, y_all.at[down, 0], y_all.at[down, 0], device(x, up, z, c))
    yc.arrived(3, y_all.at[up, 1])
    yc.start(6, y_all.at[up, 1], y_all.at[up, 1], device(x, down, z, c))
    ring_forward(wc, w_all, 3)
    ring_forward(wc, w_all, 2)
    for k, (dx, dz) in enumerate(partners):
        xc.arrived(k, x_mine.at[at(x, -dx) * 4 + at(z, -dz)])
    yc.arrived(1, y_all.at[down, 1])
    yc.arrived(2, y_all.at[up, 0])

    def half(ref, k):
        return ref.at[k * 8 : k * 8 + 8]

    def x_half(s, e, k):
        return x_all.at[s, e, k * 8 : k * 8 + 8]

    for k in (0, 1):
        xyc.start(k, half(x_mine, k), x_half(y, c, k), device(x, up, z, c))
        xyc.start(3 - k, half(x_mine, 1 - k), x_half(y, c, 1 - k), device(x, down, z, c))
    xcc.start(0, x_mine, x_all.at[y, c], device(x, y, z, twin))
    x_all[y, c] = x_mine[...]

    ring_last(wc, w_all)
    yc.arrived(4, y_all.at[y, twin])
    yc.arrived(5, y_all.at[at(y, 2), 0])
    yc.arrived(6, y_all.at[at(y, 2), 1])

    part = jnp.zeros((192, 256), F32)
    for s in range(4):
        for h in range(2):
            part += jnp.dot(
                y_all[s, :, :, h * 512 : h * 512 + 512].reshape(192, 512),
                w_all[h, 4 * s : 4 * s + 4].reshape(512, 256),
                preferred_element_type=F32,
            )
    b_part[0] = part[:, :128]
    b_part[1] = part[:, 128:]
    pc.start(0, b_part.at[twin], b_other, device(x, y, z, twin))
    pc.arrived(0, b_other)
    for h in range(2):
        b_all[h, mine] = b_part[c, h * 96 : h * 96 + 96] + b_other[h * 96 : h * 96 + 96]
    gather_first(bc, b_all)

    xyc.arrived(0, x_half(down, c, 0))
    xyc.start(4, x_half(down, c, 0), x_half(down, c, 0), device(x, up, z, c))
    xyc.arrived(3, x_half(up, c, 1))
    xyc.start(5, x_half(up, c, 1), x_half(up, c, 1), device(x, down, z, c))
    for j in (1, 3, 2):
        gather_heavy(bc, b_all, j)
    xyc.arrived(1, x_half(down, c, 1))
    xcc.start(1, x_all.at[down, c], x_all.at[down, c], device(x, y, z, twin))
    xyc.arrived(2, x_half(up, c, 0))
    xcc.start(2, x_all.at[up, c], x_all.at[up, c], device(x, y, z, twin))
    xyc.arrived(4, x_half(at(y, 2), c, 0))
    xyc.arrived(5, x_half(at(y, 2), c, 1))
    xcc.start(3, x_all.at[at(y, 2), c], x_all.at[at(y, 2), c], device(x, y, z, twin))

    def arrange(s, e):
        piece = x_all[s, e].reshape(1536, 128)
        columns = pl.ds(pl.multiple_of(s * 128, 128), 128)
        rows = pl.ds(pl.multiple_of(e * 1536, 128), 1536)
        x_full[e, :, :, :, columns] = piece.reshape(4, 4, 96, 128)
        x_flip[columns, rows] = piece.T

    for s in (y, down, up, at(y, 2)):
        arrange(s, c)
    for k, s in enumerate((y, down, up, at(y, 2))):
        xcc.arrived(k, x_all.at[s, twin])
        arrange(s, twin)

    gather_last(bc, b_all)
    bb = jnp.zeros((1, 128), F32)
    for h in range(2):
        value = b_all[h].reshape(1536, 128)
        bb += jnp.sum(value * value, axis=0, keepdims=True)
        high, low = split(value)
        b_pair[h * 1536 : h * 1536 + 1536, :128] = high
        b_pair[h * 1536 : h * 1536 + 1536, 128:] = low
    wide = jnp.dot(x_flip[...], b_pair[...], preferred_element_type=F32)
    first = wide[:, :128] + wide[:, 128:]
    u0[...] = first.reshape(4, 128, 128)
    high, low = split(first * (1.0 / TOKENS))
    u_pair[:, :128] = high
    u_pair[:, 128:] = low

    def multiply(h, d):
        rows = x_full[0, at(x, d)] if h == 0 else x_full[1, :, at(z, d)]
        wide = jnp.dot(rows.reshape(384, 512), u_pair[...], preferred_element_type=F32)
        value = (wide[:, :128] + wide[:, 128:]).reshape(4, 96, 128)
        if h == 0:
            v_part[0, at(x, d)] = value
        else:
            v_part[1, :, at(z, d)] = value

    def pair(h, d, k):
        rows = slice(2 * k, 2 * k + 2)
        return v_part.at[0, at(x, d), rows] if h == 0 else v_part.at[1, rows, at(z, d)]

    def along(h, d):
        return heavy(1 - h, d)

    for h in range(2):
        multiply(h, 2)
        vc.start(30 + h * 2, pair(h, 2, 0), v_far.at[h, 0], along(h, 1))
        vc.start(31 + h * 2, pair(h, 2, 1), v_far.at[h, 1], along(h, -1))
    for h in range(2):
        multiply(h, 1)
        vc.start(34 + h * 2, pair(h, 1, 1), v_near.at[h, 0, 2:4], along(h, 1))
        multiply(h, -1)
        vc.start(35 + h * 2, pair(h, -1, 0), v_near.at[h, 1, 0:2], along(h, -1))
    for h in range(2):
        multiply(h, 0)
    for h in range(2):
        for k, d in ((0, 1), (1, -1)):
            vc.arrived(30 + h * 2 + k, v_far.at[h, k])
            v_merge[h, k] = pair(h, d, k)[...] + v_far[h, k]
            vc.start(38 + h * 2 + k, v_merge.at[h, k], v_near.at[h, k, 2 * k : 2 * k + 2], along(h, d))

    def hand_over(copies, buf, into):
        for p in range(4):
            place = at(x, p)
            target = device(place, y, x, owner)
            if p:
                copies.start(p, buf.at[place], into.at[slot], target, lands=slot)
            else:

                @pl.when(jnp.logical_not(stays))
                def _():
                    pltpu.make_async_remote_copy(
                        src_ref=buf.at[place], dst_ref=into.at[slot], send_sem=copies.send.at[0],
                        recv_sem=copies.recv.at[slot], device_id=target, device_id_type=MESH,
                    ).start()

                @pl.when(stays)
                def _():
                    pltpu.make_async_copy(buf.at[place], into.at[slot], copies.recv.at[slot]).start()

    hand_over(uc, u0, u_in)

    for h in range(2):
        vc.arrived(34 + h * 2, v_near.at[h, 0, 2:4])
        vc.arrived(35 + h * 2, v_near.at[h, 1, 0:2])
        vc.arrived(38 + h * 2, v_near.at[h, 0, 0:2])
        vc.arrived(39 + h * 2, v_near.at[h, 1, 2:4])
        own = v_part[0, x] if h == 0 else v_part[1, :, z]
        v_sum[h] = own + v_near[h, 0] + v_near[h, 1]
        for d in (1, 3, 2):
            lane = at(z, d) if h == 0 else at(x, d)
            vc.start(42 + h * 3 + d - 1, v_sum.at[h, lane], v_light.at[h, d - 1], light(1 - h, d))
    for h in range(2):
        for d in (1, 3, 2):
            vc.arrived(42 + h * 3 + d - 1, v_light.at[h, d - 1])
        lane = z if h == 0 else x
        v_all[h, mine] = v_sum[h, lane] + v_light[h, 0] + v_light[h, 1] + v_light[h, 2]
    gather_first(vc, v_all)
    for j in (1, 3, 2):
        gather_heavy(vc, v_all, j)
    gather_last(vc, v_all)

    bv = jnp.zeros((1, 128), F32)
    for h in range(2):
        bv += jnp.sum((b_all[h] * v_all[h]).reshape(1536, 128), axis=0, keepdims=True)
    alpha = bb / (bv + RIDGE * bb)
    norm = jnp.zeros((1, 128), F32)
    for h in range(2):
        value = b_all[h].reshape(1536, 128)
        residual = value - alpha * (v_all[h].reshape(1536, 128) + RIDGE * value)
        norm += jnp.sum(residual * residual, axis=0, keepdims=True)
        r_all[h] = residual
        high, low = split(residual)
        b_pair[h * 1536 : h * 1536 + 1536, :128] = high
        b_pair[h * 1536 : h * 1536 + 1536, 128:] = low
    beta = norm / bb
    wide = jnp.dot(x_flip[...], b_pair[...], preferred_element_type=F32)
    turned = wide[:, :128] + wide[:, 128:] + beta * u0[...].reshape(512, 128)
    ud[...] = turned.reshape(4, 128, 128)
    gamma[mine] = jnp.broadcast_to(jnp.sum(turned * turned, axis=0, keepdims=True), (8, 128))
    for k, (dx, dz) in enumerate(partners):
        gc.start(k, gamma.at[mine], gamma.at[mine], device(at(x, dx), y, at(z, dz), c))
    hand_over(dc, ud, d_in)
    dd = jnp.zeros((1, 128), F32)
    for h in range(2):
        turn = r_all[h] + beta * b_all[h].reshape(1536, 128)
        dd += jnp.sum(turn * turn, axis=0, keepdims=True)
    for k, (dx, dz) in enumerate(partners):
        gc.arrived(k, gamma.at[at(x, -dx) * 4 + at(z, -dz)])
    curve = jnp.sum(gamma[...], axis=0)[:1] * (1.0 / TOKENS) + RIDGE * dd
    step = norm / curve
    scalars[c] = jnp.concatenate(
        [jnp.broadcast_to(alpha * (1.0 / TOKENS), (8, 128)), jnp.broadcast_to(step * (1.0 / TOKENS), (8, 128))], axis=0
    )
    tc.start(0, scalars.at[c], scalars.at[c], device(x, y, z, twin))
    for k in range(4):
        uc.arrived(k, u_in.at[k])
        dc.arrived(k, d_in.at[k])
    tc.arrived(0, scalars.at[twin])
    for k in range(4):
        t, e = k // 2, k % 2
        out_ref[t * 128 : t * 128 + 128, e * 128 : e * 128 + 128] = (
            scalars[e, 0:1] * u_in[k] + scalars[e, 8:9] * d_in[k]
        )

    @pl.when(jnp.logical_not(stays))
    def _():
        pltpu.make_async_copy(u0.at[0], u0.at[0], u_s.at[0]).wait()
        pltpu.make_async_copy(ud.at[0], ud.at[0], d_s.at[0]).wait()

    for copies in (wc, yc, xc, bc, vc, xyc, xcc, pc, gc, tc, uc, dc):
        copies.finish()


def local(activations, targets, key_weight):
    dma = pltpu.SemaphoreType.DMA
    buffers = [
        ((16, 96, 128), BF16),
        ((2, 96, 1024), BF16),
        ((4, 2, 96, 1024), BF16),
        ((2, 16, 128, 256), BF16),
        ((16, 96, 128), BF16),
        ((4, 2, 16, 96, 128), BF16),
        ((2, 4, 4, 96, 512), BF16),
        ((512, TOKENS), BF16),
        ((2, 192, 128), F32),
        ((192, 128), F32),
        ((2, 16, 96, 128), F32),
        ((TOKENS, 256), BF16),
        ((4, 128, 128), F32),
        ((512, 256), BF16),
        ((4, 128, 128), F32),
        ((2, 4, 4, 96, 128), F32),
        ((2, 2, 2, 96, 128), F32),
        ((2, 2, 2, 96, 128), F32),
        ((2, 2, 4, 96, 128), F32),
        ((2, 4, 96, 128), F32),
        ((2, 3, 96, 128), F32),
        ((2, 16, 96, 128), F32),
        ((2, 1536, 128), F32),
        ((16, 8, 128), F32),
        ((2, 16, 128), F32),
        ((4, 128, 128), F32),
        ((4, 128, 128), F32),
    ]
    counts = (7, 30, 15, 6, 4, 1, 30, 48, 15, 1, 4, 4)
    return pl.pallas_call(
        kernel,
        out_shape=jax.ShapeDtypeStruct((256, 256), F32),
        in_specs=[pl.BlockSpec(memory_space=pl.ANY)] * 3,
        out_specs=pl.BlockSpec(memory_space=pltpu.VMEM),
        scratch_shapes=[pltpu.VMEM(*b) for b in buffers] + [dma((34,))] + [dma((n,)) for n in counts for _ in range(2)],
        compiler_params=pltpu.CompilerParams(collective_id=0, has_side_effects=True, vmem_limit_bytes=56 * 2**20),
    )(activations, targets, key_weight)


def solution(mesh):
    placed = (P("dp", "tensor"), P("dp", "tensor"), P("dp", "tensor"))
    return jax.shard_map(local, mesh=mesh, in_specs=placed, out_specs=P("dp", "tensor"), check_vma=False)
```

```python
import jax
import jax.numpy as jnp
from jax import lax
from jax.experimental import pallas as pl
from jax.experimental.pallas import tpu as pltpu
from jax.sharding import PartitionSpec as P

MESH = pl.DeviceIdType.MESH
TOKENS = 3072
RIDGE = 0.5
F32, BF16 = jnp.float32, jnp.bfloat16


def device(x, y, z, c):
    return (x * 8 + z * 2 + c, y)


def split(value):
    high = value.astype(BF16)
    return high, (value - high.astype(F32)).astype(BF16)


def encode(value):
    top = jnp.max(jnp.abs(value), axis=-2, keepdims=True)
    scale = jnp.maximum(top * 1.03125, 1e-30).astype(BF16)
    inverse = 8.0 / scale.astype(F32)
    p = jnp.abs(value) * inverse + 0.125
    p = p * p
    p = p * p
    p8 = p * p
    p = p8 * p8
    p = p * p * p8
    code = jnp.where(value < 0, -p, p).astype(BF16)
    return code, jnp.broadcast_to(scale, scale.shape[:-2] + (16, 128))


def decode(ref):
    code = ref[..., :96, :].astype(F32)
    scale = ref[..., 96:112, :].astype(F32)[..., :1, :] * 0.125
    p = jnp.exp2(jnp.log2(jnp.abs(code)) * (1.0 / 40.0))
    value = (p - 0.125) * scale
    return jnp.where(code < 0, -value, value)


def keep(ref, value):
    ref[..., :96, :], ref[..., 96:112, :] = encode(value)


class Copies:
    def __init__(self, send, recv):
        self.send, self.recv, self.started = send, recv, []

    def start(self, index, src, dst, target, lands=None):
        copy = pltpu.make_async_remote_copy(
            src_ref=src,
            dst_ref=dst,
            send_sem=self.send.at[index],
            recv_sem=self.recv.at[index if lands is None else lands],
            device_id=target,
            device_id_type=MESH,
        )
        copy.start()
        self.started.append(copy)
        return copy

    def arrived(self, index, dst):
        pltpu.make_async_copy(dst, dst, self.recv.at[index]).wait()

    def finish(self):
        for copy in self.started:
            copy.wait_send()


def kernel(
    x_in, y_in, w_in, out_ref,
    x_sort, y_sort, y_all, w_all, x_mine, x_all, x_full, x_flip,
    b_part, b_other, b_code, b_all, b_pair, u0, u_pair, ud,
    v_own, v_part, v_near, v_sum, v_send, v_light, v_code, v_all, r_all, gamma, scalars, u_in, d_in,
    l_s, y_s, y_r, w_s, w_r, x_s, x_r, xy_s, xy_r, xc_s, xc_r, p_s, p_r,
    b_s, b_r, v_s, v_r, g_s, g_r, t_s, t_r, u_s, u_r, d_s, d_r,
):
    i = lax.axis_index("dp")
    y = lax.axis_index("tensor")
    x, z, c = i // 8, lax.rem(i // 2, 4), lax.rem(i, 2)
    mine = x * 4 + z
    twin = 1 - c

    def at(a, d):
        return lax.rem(a + d + 4, 4)

    partners = [(dx, dz) for dx in range(4) for dz in range(4) if dx or dz]
    up, down = at(y, 1), at(y, -1)

    slot = lax.rem(z, 2) * 2 + c
    owner = z // 2
    stays = jnp.logical_and(x == z, owner == c)
    barrier = pltpu.get_barrier_semaphore()
    peers = [device(at(x, dx), y, at(z, dz), c) for dx, dz in partners]
    peers += [device(at(x, dx), y, at(z, dz), twin) for dx in range(4) for dz in range(4)]
    peers += [device(x, at(y, d), z, c) for d in (1, 2, 3)]
    peers += [device(x, place, z, twin) for place in (up, down)]
    for peer in peers:
        pl.semaphore_signal(barrier, inc=1, device_id=peer, device_id_type=MESH)

    loads = []
    for h in range(2):
        loads.append((w_in.at[h * 128 : h * 128 + 128, :], w_all.at[h, mine]))
    for e in range(2):
        for h in range(2):
            for q in range(4):
                columns = slice(q * 512 + e * 256 + h * 128, q * 512 + e * 256 + h * 128 + 128)
                loads.append((y_in.at[:, columns], y_sort.at[e, :, h * 512 + q * 128 : h * 512 + q * 128 + 128]))
    for k in range(16):
        loads.append((x_in.at[:, k * 128 : k * 128 + 128], x_sort.at[k]))
    loads = [pltpu.make_async_copy(src, dst, l_s.at[k]) for k, (src, dst) in enumerate(loads)]
    for load in loads:
        load.start()
    for load in loads[:2]:
        load.wait()
    pl.semaphore_wait(barrier, len(peers))

    wc, yc, xc, xyc, xcc = Copies(w_s, w_r), Copies(y_s, y_r), Copies(x_s, x_r), Copies(xy_s, xy_r), Copies(xc_s, xc_r)
    pc, bc, vc = Copies(p_s, p_r), Copies(b_s, b_r), Copies(v_s, v_r)
    gc, tc, uc, dc = Copies(g_s, g_r), Copies(t_s, t_r), Copies(u_s, u_r), Copies(d_s, d_r)

    def light(h, d):
        return device(at(x, d), y, z, c) if h == 0 else device(x, y, at(z, d), c)

    def heavy(h, d):
        return device(x, y, at(z, d), c) if h == 0 else device(at(x, d), y, z, c)

    def block(h, dl, dh):
        return at(x, dl) * 4 + at(z, dh) if h == 0 else at(x, dh) * 4 + at(z, dl)

    def gather_first(copies, buf):
        for d in (1, 3, 2):
            for h in range(2):
                copies.start(h * 3 + d - 1, buf.at[h, mine], buf.at[h, mine], light(h, d))
        gather_heavy(copies, buf, 0)

    def gather_heavy(copies, buf, j):
        for h in range(2):
            part = buf.at[h, block(h, -j, 0)]
            if j:
                copies.arrived(h * 3 + j - 1, part)
            for d in (1, 3, 2):
                copies.start(6 + h * 12 + j * 3 + d - 1, part, part, heavy(h, d))

    def gather_rest(copies, buf, use):
        for j in (1, 3, 2):
            gather_heavy(copies, buf, j)
        for h in range(2):
            for j in (0, 1, 3, 2):
                use(h, block(h, -j, 0))

    def gather_last(copies, buf, use):
        for j in (0, 1, 3, 2):
            for h in range(2):
                for d in (1, 3, 2):
                    place = block(h, -j, -d)
                    copies.arrived(6 + h * 12 + j * 3 + d - 1, buf.at[h, place])
                    use(h, place)

    gather_first(wc, w_all)

    def send_y(e, flip):
        target = lax.rem(c + e, 2)
        place = lax.rem(y + 1 + 2 * lax.rem(c + flip, 2), 4)
        return yc.start(flip * 2 + e, y_sort.at[target], y_all.at[y, c], device(x, place, z, target), lands=flip * 2 + c)

    for load in loads[2:18]:
        load.wait()
    first = [send_y(e, 0) for e in range(2)]
    for load in loads[18:]:
        load.wait()
    for k, (dx, dz) in enumerate(partners):
        xc.start(k, x_sort.at[at(x, dx) * 4 + at(z, dz)], x_mine.at[mine], device(at(x, dx), y, at(z, dz), c))
    y_all[y, c] = y_sort[c]
    x_mine[mine] = x_sort[mine]
    for copy in first:
        copy.wait_send()
        yc.started.remove(copy)
    for e in range(2):
        send_y(e, 1)
    yc.start(4, y_sort.at[twin], y_all.at[y, c], device(x, y, z, twin))

    for j in (1, 3, 2):
        gather_heavy(wc, w_all, j)
    yc.arrived(0, y_all.at[down, 0])
    yc.start(5, y_all.at[down, 0], y_all.at[down, 0], device(x, up, z, c))
    yc.arrived(1, y_all.at[up, 1])
    yc.start(6, y_all.at[up, 1], y_all.at[up, 1], device(x, down, z, c))
    for k, (dx, dz) in enumerate(partners):
        xc.arrived(k, x_mine.at[at(x, -dx) * 4 + at(z, -dz)])

    def x_half(s, e, k):
        return x_all.at[s, e, k * 8 : k * 8 + 8]

    def send_x(k, flip):
        place = up if k == flip else down
        xyc.start(flip * 2 + k, x_mine.at[k * 8 : k * 8 + 8], x_half(y, c, k), device(x, place, z, c))

    for k in range(2):
        send_x(k, 0)
    xcc.start(0, x_mine, x_all.at[y, c], device(x, y, z, twin))
    x_all[y, c] = x_mine[...]
    xyc.arrived(0, x_half(down, c, 0))
    xyc.start(4, x_half(down, c, 0), x_half(down, c, 0), device(x, up, z, c))
    xyc.arrived(1, x_half(up, c, 1))
    xyc.start(5, x_half(up, c, 1), x_half(up, c, 1), device(x, down, z, c))
    for k in range(2):
        send_x(k, 1)

    for h in range(2):
        for j in (0, 1, 3, 2):
            for d in (1, 3, 2):
                wc.arrived(6 + h * 12 + j * 3 + d - 1, w_all.at[h, block(h, -j, -d)])
    yc.arrived(2, y_all.at[up, 0])
    yc.arrived(3, y_all.at[down, 1])
    yc.arrived(4, y_all.at[y, twin])
    yc.arrived(5, y_all.at[at(y, 2), 0])
    yc.arrived(6, y_all.at[at(y, 2), 1])

    part = jnp.zeros((192, 256), F32)
    for s in range(4):
        for h in range(2):
            part += jnp.dot(
                y_all[s, :, :, h * 512 : h * 512 + 512].reshape(192, 512),
                w_all[h, 4 * s : 4 * s + 4].reshape(512, 256),
                preferred_element_type=F32,
            )
    b_part[0] = part[:, :128]
    b_part[1] = part[:, 128:]
    pc.start(0, b_part.at[twin], b_other, device(x, y, z, twin))
    pc.arrived(0, b_other)
    for h in range(2):
        keep(b_code.at[h, mine], b_part[c, h * 96 : h * 96 + 96] + b_other[h * 96 : h * 96 + 96])
    gather_first(bc, b_code)

    norms = []

    def use_b(h, place):
        value = decode(b_code.at[h, place])
        b_all[h, place] = value
        norms.append(jnp.sum(value * value, axis=0, keepdims=True))
        high, low = split(value)
        b_pair[h, place, :, :128] = high
        b_pair[h, place, :, 128:] = low

    gather_rest(bc, b_code, use_b)
    xyc.arrived(2, x_half(up, c, 0))
    xcc.start(3, x_all.at[up, c], x_all.at[up, c], device(x, y, z, twin))
    xyc.arrived(3, x_half(down, c, 1))
    xcc.start(1, x_all.at[down, c], x_all.at[down, c], device(x, y, z, twin))
    xyc.arrived(4, x_half(at(y, 2), c, 0))
    xyc.arrived(5, x_half(at(y, 2), c, 1))
    xcc.start(2, x_all.at[at(y, 2), c], x_all.at[at(y, 2), c], device(x, y, z, twin))

    def arrange(s, e):
        piece = x_all[s, e].reshape(1536, 128)
        columns = pl.ds(pl.multiple_of(s * 128, 128), 128)
        rows = pl.ds(pl.multiple_of(e * 1536, 128), 1536)
        x_full[e, :, :, :, columns] = piece.reshape(4, 4, 96, 128)
        x_flip[columns, rows] = piece.T

    for d in (0, 1, 3, 2):
        arrange(at(y, -d), c)
    for d in (0, 1, 3, 2):
        xcc.arrived(d, x_all.at[at(y, -d), twin])
        arrange(at(y, -d), twin)

    gather_last(bc, b_code, use_b)
    bb = sum(norms)
    wide = jnp.dot(x_flip[...], b_pair[...].reshape(TOKENS, 256), preferred_element_type=F32)
    first = wide[:, :128] + wide[:, 128:]
    u0[...] = first.reshape(4, 128, 128)
    high, low = split(first * (1.0 / TOKENS))
    u_pair[:, :128] = high
    u_pair[:, 128:] = low

    def multiply(h, d):
        rows = x_full[0, at(x, d)] if h == 0 else x_full[1, :, at(z, d)]
        wide = jnp.dot(rows.reshape(384, 512), u_pair[...], preferred_element_type=F32)
        value = (wide[:, :128] + wide[:, 128:]).reshape(4, 96, 128)
        if d == 0:
            v_own[h] = value
        else:
            keep(v_part.at[h, d - 1], value)
            vc.start(30 + h * 3 + d - 1, v_part.at[h, d - 1], v_near.at[h, d - 1], heavy(1 - h, d))

    for d in (2, 1, 3, 0):
        for h in range(2):
            multiply(h, d)

    def hand_over(copies, buf, into):
        for p in range(4):
            place = at(x, p)
            target = device(place, y, x, owner)
            if p:
                copies.start(p, buf.at[place], into.at[slot], target, lands=slot)
            else:

                @pl.when(jnp.logical_not(stays))
                def _():
                    pltpu.make_async_remote_copy(
                        src_ref=buf.at[place], dst_ref=into.at[slot], send_sem=copies.send.at[0],
                        recv_sem=copies.recv.at[slot], device_id=target, device_id_type=MESH,
                    ).start()

                @pl.when(stays)
                def _():
                    pltpu.make_async_copy(buf.at[place], into.at[slot], copies.recv.at[slot]).start()

    hand_over(uc, u0, u_in)

    for h in range(2):
        total = v_own[h]
        for d in (1, 3, 2):
            vc.arrived(30 + h * 3 + d - 1, v_near.at[h, d - 1])
            total += decode(v_near.at[h, d - 1])
        v_sum[h] = total
        keep(v_send.at[h], total)
        for d in (1, 3, 2):
            lane = at(z, d) if h == 0 else at(x, d)
            vc.start(36 + h * 3 + d - 1, v_send.at[h, lane], v_light.at[h, d - 1], light(1 - h, d))
    for h in range(2):
        total = v_sum[h, z if h == 0 else x]
        for d in (1, 3, 2):
            vc.arrived(36 + h * 3 + d - 1, v_light.at[h, d - 1])
            total += decode(v_light.at[h, d - 1])
        keep(v_code.at[h, mine], total)
    gather_first(vc, v_code)

    dots = []

    def use_v(h, place):
        value = decode(v_code.at[h, place])
        v_all[h, place] = value
        dots.append(jnp.sum(value * b_all[h, place], axis=0, keepdims=True))

    gather_rest(vc, v_code, use_v)
    gather_last(vc, v_code, use_v)

    bv = sum(dots)
    alpha = bb / (bv + RIDGE * bb)
    norm = jnp.zeros((1, 128), F32)
    for h in range(2):
        value = b_all[h].reshape(1536, 128)
        residual = value - alpha * (v_all[h].reshape(1536, 128) + RIDGE * value)
        norm += jnp.sum(residual * residual, axis=0, keepdims=True)
        r_all[h] = residual
        high, low = split(residual)
        b_pair[h, :, :, :128] = high.reshape(16, 96, 128)
        b_pair[h, :, :, 128:] = low.reshape(16, 96, 128)
    beta = norm / bb
    wide = jnp.dot(x_flip[...], b_pair[...].reshape(TOKENS, 256), preferred_element_type=F32)
    turned = wide[:, :128] + wide[:, 128:] + beta * u0[...].reshape(512, 128)
    ud[...] = turned.reshape(4, 128, 128)
    gamma[c, mine] = jnp.broadcast_to(jnp.sum(turned * turned, axis=0, keepdims=True), (8, 128))
    spread = [(dx, dz, e) for dx in (2, 1, 3, 0) for dz in (2, 1, 3, 0) for e in (0, 1) if dx or dz or e]
    for k, (dx, dz, e) in enumerate(spread):
        gc.start(k, gamma.at[c, mine], gamma.at[c, mine], device(at(x, dx), y, at(z, dz), lax.rem(c + e, 2)))
    hand_over(dc, ud, d_in)
    dd = jnp.zeros((1, 128), F32)
    for h in range(2):
        turn = r_all[h] + beta * b_all[h].reshape(1536, 128)
        dd += jnp.sum(turn * turn, axis=0, keepdims=True)
    scalars[c, 0] = jnp.broadcast_to(alpha * (1.0 / TOKENS), (8, 128))
    scalars[c, 1] = jnp.broadcast_to(norm * (1.0 / TOKENS), (8, 128))
    scalars[c, 2] = jnp.broadcast_to(dd * RIDGE, (8, 128))
    tc.start(0, scalars.at[c], scalars.at[c], device(x, y, z, twin))
    tc.arrived(0, scalars.at[twin])
    for k, (dx, dz, e) in enumerate(spread):
        gc.arrived(k, gamma.at[lax.rem(c + e, 2), at(x, -dx) * 4 + at(z, -dz)])
    steps = []
    for e in range(2):
        curve = jnp.sum(gamma[e], axis=0)[:1] * (1.0 / TOKENS) + scalars[e, 2, :1]
        steps.append(scalars[e, 1, :1] / curve)
    for k in range(4):
        uc.arrived(k, u_in.at[k])
        dc.arrived(k, d_in.at[k])
    for k in range(4):
        t, e = k // 2, k % 2
        out_ref[t * 128 : t * 128 + 128, e * 128 : e * 128 + 128] = (
            scalars[e, 0, :1] * u_in[k] + steps[e] * d_in[k]
        )

    @pl.when(jnp.logical_not(stays))
    def _():
        pltpu.make_async_copy(u0.at[0], u0.at[0], u_s.at[0]).wait()
        pltpu.make_async_copy(ud.at[0], ud.at[0], d_s.at[0]).wait()

    for copies in (wc, yc, xc, bc, vc, xyc, xcc, pc, gc, tc, uc, dc):
        copies.finish()


def local(activations, targets, key_weight):
    dma = pltpu.SemaphoreType.DMA
    buffers = [
        ((16, 96, 128), BF16),
        ((2, 96, 1024), BF16),
        ((4, 2, 96, 1024), BF16),
        ((2, 16, 128, 256), BF16),
        ((16, 96, 128), BF16),
        ((4, 2, 16, 96, 128), BF16),
        ((2, 4, 4, 96, 512), BF16),
        ((512, TOKENS), BF16),
        ((2, 192, 128), F32),
        ((192, 128), F32),
        ((2, 16, 112, 128), BF16),
        ((2, 16, 96, 128), F32),
        ((2, 16, 96, 256), BF16),
        ((4, 128, 128), F32),
        ((512, 256), BF16),
        ((4, 128, 128), F32),
        ((2, 4, 96, 128), F32),
        ((2, 3, 4, 112, 128), BF16),
        ((2, 3, 4, 112, 128), BF16),
        ((2, 4, 96, 128), F32),
        ((2, 4, 112, 128), BF16),
        ((2, 3, 112, 128), BF16),
        ((2, 16, 112, 128), BF16),
        ((2, 16, 96, 128), F32),
        ((2, 1536, 128), F32),
        ((2, 16, 8, 128), F32),
        ((2, 3, 8, 128), F32),
        ((4, 128, 128), F32),
        ((4, 128, 128), F32),
    ]
    counts = (7, 30, 15, 6, 4, 1, 30, 42, 31, 1, 4, 4)
    return pl.pallas_call(
        kernel,
        out_shape=jax.ShapeDtypeStruct((256, 256), F32),
        in_specs=[pl.BlockSpec(memory_space=pl.ANY)] * 3,
        out_specs=pl.BlockSpec(memory_space=pltpu.VMEM),
        scratch_shapes=[pltpu.VMEM(*b) for b in buffers] + [dma((34,))] + [dma((n,)) for n in counts for _ in range(2)],
        compiler_params=pltpu.CompilerParams(collective_id=0, has_side_effects=True, vmem_limit_bytes=56 * 2**20),
    )(activations, targets, key_weight)


def solution(mesh):
    placed = (P("dp", "tensor"), P("dp", "tensor"), P("dp", "tensor"))
    return jax.shard_map(local, mesh=mesh, in_specs=placed, out_specs=P("dp", "tensor"), check_vma=False)
```

```python
import jax
import jax.numpy as jnp
from jax import lax
from jax.experimental import pallas as pl
from jax.experimental.pallas import tpu as pltpu
from jax.sharding import PartitionSpec as P

MESH = pl.DeviceIdType.MESH
TOKENS = 3072
RIDGE = 0.5
F32, BF16 = jnp.float32, jnp.bfloat16


def device(x, y, z, c):
    return (x * 8 + z * 2 + c, y)


def split(value):
    high = value.astype(BF16)
    return high, (value - high.astype(F32)).astype(BF16)


def encode(value):
    top = jnp.max(jnp.abs(value), axis=-2, keepdims=True)
    scale = jnp.maximum(top * 1.03125, 1e-30).astype(BF16)
    inverse = 8.0 / scale.astype(F32)
    p = jnp.abs(value) * inverse + 0.125
    p = p * p
    p = p * p
    p8 = p * p
    p = p8 * p8
    p = p * p * p8
    code = jnp.where(value < 0, -p, p).astype(BF16)
    return code, jnp.broadcast_to(scale, scale.shape[:-2] + (16, 128))


def decode(ref):
    rows = ref.shape[-2] - 16
    code = ref[..., :rows, :].astype(F32)
    scale = ref[..., rows:, :].astype(F32)[..., :1, :] * 0.125
    p = jnp.exp2(jnp.log2(jnp.abs(code)) * (1.0 / 40.0))
    value = (p - 0.125) * scale
    return jnp.where(code < 0, -value, value)


def keep(ref, value):
    rows = value.shape[-2]
    ref[..., :rows, :], ref[..., rows:, :] = encode(value)


class Copies:
    def __init__(self, send, recv):
        self.send, self.recv, self.started = send, recv, []

    def start(self, index, src, dst, target, lands=None):
        copy = pltpu.make_async_remote_copy(
            src_ref=src,
            dst_ref=dst,
            send_sem=self.send.at[index],
            recv_sem=self.recv.at[index if lands is None else lands],
            device_id=target,
            device_id_type=MESH,
        )
        copy.start()
        self.started.append(copy)

    def arrived(self, index, dst):
        pltpu.make_async_copy(dst, dst, self.recv.at[index]).wait()

    def finish(self):
        for copy in self.started:
            copy.wait_send()


def kernel(
    x_in, y_in, w_in, out_ref,
    x_sort, y_sort, y_all, w_all, x_mine, x_all, x_full, x_flip,
    b_part, b_other, b_code, b_all, b_pair, u0, u_pair, u_code, d_code,
    v_own, v_part, v_near, v_send, v_line, v_code, v_all, r_all, gamma, scalars, u_in, d_in,
    l_s, y_s, y_r, w_s, w_r, x_s, x_r, xy_s, xy_r, xc_s, xc_r, p_s, p_r,
    b_s, b_r, v_s, v_r, g_s, g_r, t_s, t_r, u_s, u_r, d_s, d_r,
):
    i = lax.axis_index("dp")
    y = lax.axis_index("tensor")
    x, z, c = i // 8, lax.rem(i // 2, 4), lax.rem(i, 2)
    mine = x * 4 + z
    twin = 1 - c

    def at(a, d):
        return lax.rem(a + d + 4, 4)

    partners = [(dx, dz) for dx in range(4) for dz in range(4) if dx or dz]
    up, down = at(y, 1), at(y, -1)

    slot = lax.rem(z, 2) * 2 + c
    owner = z // 2
    stays = jnp.logical_and(x == z, owner == c)
    barrier = pltpu.get_barrier_semaphore()
    peers = [device(at(x, dx), y, at(z, dz), c) for dx, dz in partners]
    peers += [device(at(x, dx), y, at(z, dz), twin) for dx in range(4) for dz in range(4)]
    peers += [device(x, at(y, d), z, c) for d in (1, 2, 3)]
    peers += [device(x, place, z, twin) for place in (up, down)]
    for peer in peers:
        pl.semaphore_signal(barrier, inc=1, device_id=peer, device_id_type=MESH)

    loads = []
    for h in range(2):
        loads.append((w_in.at[h * 128 : h * 128 + 128, :], w_all.at[h, mine]))
    for e in range(2):
        for h in range(2):
            for q in range(4):
                columns = slice(q * 512 + e * 256 + h * 128, q * 512 + e * 256 + h * 128 + 128)
                loads.append((y_in.at[:, columns], y_sort.at[e, :, h * 512 + q * 128 : h * 512 + q * 128 + 128]))
    for k in range(16):
        loads.append((x_in.at[:, k * 128 : k * 128 + 128], x_sort.at[k]))
    loads = [pltpu.make_async_copy(src, dst, l_s.at[k]) for k, (src, dst) in enumerate(loads)]
    for load in loads:
        load.start()
    for load in loads:
        load.wait()
    pl.semaphore_wait(barrier, len(peers))

    wc, yc, xc, xyc, xcc = Copies(w_s, w_r), Copies(y_s, y_r), Copies(x_s, x_r), Copies(xy_s, xy_r), Copies(xc_s, xc_r)
    pc, bc, vc = Copies(p_s, p_r), Copies(b_s, b_r), Copies(v_s, v_r)
    gc, tc, uc, dc = Copies(g_s, g_r), Copies(t_s, t_r), Copies(u_s, u_r), Copies(d_s, d_r)

    def light(h, d):
        return device(at(x, d), y, z, c) if h == 0 else device(x, y, at(z, d), c)

    def heavy(h, d):
        return device(x, y, at(z, d), c) if h == 0 else device(at(x, d), y, z, c)

    def block(h, dl, dh):
        return at(x, dl) * 4 + at(z, dh) if h == 0 else at(x, dh) * 4 + at(z, dl)

    def gather_first(copies, buf):
        for d in (1, 3, 2):
            for h in range(2):
                copies.start(h * 3 + d - 1, buf.at[h, mine], buf.at[h, mine], light(h, d))
        gather_heavy(copies, buf, 0)

    def gather_heavy(copies, buf, j):
        for h in range(2):
            part = buf.at[h, block(h, -j, 0)]
            if j:
                copies.arrived(h * 3 + j - 1, part)
            for d in (1, 3, 2):
                copies.start(6 + h * 12 + j * 3 + d - 1, part, part, heavy(h, d))

    def gather_rest(copies, buf, use):
        for j in (1, 3, 2):
            gather_heavy(copies, buf, j)
        for h in range(2):
            for j in (0, 1, 3, 2):
                use(h, block(h, -j, 0))

    def gather_last(copies, buf, use):
        for j in (0, 1, 3, 2):
            for h in range(2):
                for d in (1, 3, 2):
                    place = block(h, -j, -d)
                    copies.arrived(6 + h * 12 + j * 3 + d - 1, buf.at[h, place])
                    use(h, place)

    def ring_heavy(j):
        for h in range(2):
            part = w_all.at[h, block(h, -j, 0)]
            if j:
                wc.arrived(h * 3 + j - 1, part)
            wc.start(6 + h * 8 + j * 2, part, part, heavy(h, 1))
            wc.start(6 + h * 8 + j * 2 + 1, part, part, heavy(h, -1))

    def ring_forward(j):
        for h in range(2):
            k, d = (0, 1) if j in (0, 1) else (1, -1)
            part = w_all.at[h, block(h, -j, -d)]
            wc.arrived(6 + h * 8 + j * 2 + k, part)
            wc.start(22 + h * 4 + j, part, part, heavy(h, d))

    for k, (dx, dz) in enumerate(partners):
        xc.start(k, x_sort.at[at(x, dx) * 4 + at(z, dz)], x_mine.at[mine], device(at(x, dx), y, at(z, dz), c))

    for flip in range(2):
        for e in range(2):
            target = lax.rem(c + e, 2)
            place = lax.rem(y + 1 + 2 * lax.rem(c + flip, 2), 4)
            yc.start(flip * 2 + e, y_sort.at[target], y_all.at[y, c], device(x, place, z, target), lands=flip * 2 + c)
    for d in (1, 3, 2):
        for h in range(2):
            wc.start(h * 3 + d - 1, w_all.at[h, mine], w_all.at[h, mine], light(h, d))
    ring_heavy(0)
    yc.start(4, y_sort.at[twin], y_all.at[y, c], device(x, y, z, twin))
    y_all[y, c] = y_sort[c]
    x_mine[mine] = x_sort[mine]

    yc.arrived(0, y_all.at[down, 0])
    yc.start(5, y_all.at[down, 0], y_all.at[down, 0], device(x, up, z, c))
    yc.arrived(1, y_all.at[up, 1])
    yc.start(6, y_all.at[up, 1], y_all.at[up, 1], device(x, down, z, c))
    for k, (dx, dz) in enumerate(partners):
        xc.arrived(k, x_mine.at[at(x, -dx) * 4 + at(z, -dz)])

    def x_half(s, e, k):
        return x_all.at[s, e, k * 8 : k * 8 + 8]

    for flip in range(2):
        for k in range(2):
            place = up if k == flip else down
            xyc.start(flip * 2 + k, x_mine.at[k * 8 : k * 8 + 8], x_half(y, c, k), device(x, place, z, c))
    xcc.start(0, x_mine, x_all.at[y, c], device(x, y, z, twin))
    for j in (1, 3, 2):
        ring_heavy(j)
    x_all[y, c] = x_mine[...]
    for j in (0, 1, 3, 2):
        ring_forward(j)
    xyc.arrived(0, x_half(down, c, 0))
    xyc.start(4, x_half(down, c, 0), x_half(down, c, 0), device(x, up, z, c))
    xyc.arrived(1, x_half(up, c, 1))
    xyc.start(5, x_half(up, c, 1), x_half(up, c, 1), device(x, down, z, c))
    for h in range(2):
        for j in (2, 3):
            wc.arrived(6 + h * 8 + j * 2, w_all.at[h, block(h, -j, -1)])
        for j in (0, 1):
            wc.arrived(6 + h * 8 + j * 2 + 1, w_all.at[h, block(h, -j, 1)])
        for j in range(4):
            wc.arrived(22 + h * 4 + j, w_all.at[h, block(h, -j, 2)])
    yc.arrived(2, y_all.at[up, 0])
    yc.arrived(3, y_all.at[down, 1])
    yc.arrived(4, y_all.at[y, twin])
    yc.arrived(5, y_all.at[at(y, 2), 0])
    yc.arrived(6, y_all.at[at(y, 2), 1])

    part = jnp.zeros((192, 256), F32)
    for s in range(4):
        for h in range(2):
            part += jnp.dot(
                y_all[s, :, :, h * 512 : h * 512 + 512].reshape(192, 512),
                w_all[h, 4 * s : 4 * s + 4].reshape(512, 256),
                preferred_element_type=F32,
            )
    b_part[0] = part[:, :128]
    b_part[1] = part[:, 128:]
    pc.start(0, b_part.at[twin], b_other, device(x, y, z, twin))
    pc.arrived(0, b_other)
    for h in range(2):
        keep(b_code.at[h, mine], b_part[c, h * 96 : h * 96 + 96] + b_other[h * 96 : h * 96 + 96])
    gather_first(bc, b_code)

    norms = []

    def use_b(h, place):
        value = decode(b_code.at[h, place])
        b_all[h, place] = value
        norms.append(jnp.sum(value * value, axis=0, keepdims=True))
        high, low = split(value)
        b_pair[h, place, :, :128] = high
        b_pair[h, place, :, 128:] = low

    gather_rest(bc, b_code, use_b)
    xyc.arrived(2, x_half(up, c, 0))
    xcc.start(3, x_all.at[up, c], x_all.at[up, c], device(x, y, z, twin))
    xyc.arrived(3, x_half(down, c, 1))
    xcc.start(1, x_all.at[down, c], x_all.at[down, c], device(x, y, z, twin))
    xyc.arrived(4, x_half(at(y, 2), c, 0))
    xyc.arrived(5, x_half(at(y, 2), c, 1))
    xcc.start(2, x_all.at[at(y, 2), c], x_all.at[at(y, 2), c], device(x, y, z, twin))

    def arrange(s, e):
        piece = x_all[s, e].reshape(1536, 128)
        columns = pl.ds(pl.multiple_of(s * 128, 128), 128)
        rows = pl.ds(pl.multiple_of(e * 1536, 128), 1536)
        x_full[e, :, :, :, columns] = piece.reshape(4, 4, 96, 128)
        x_flip[columns, rows] = piece.T

    for d in (0, 1, 3, 2):
        arrange(at(y, -d), c)
    for d in (0, 1, 3, 2):
        xcc.arrived(d, x_all.at[at(y, -d), twin])
        arrange(at(y, -d), twin)

    gather_last(bc, b_code, use_b)
    bb = sum(norms)
    wide = jnp.dot(x_flip[...], b_pair[...].reshape(TOKENS, 256), preferred_element_type=F32)
    first = wide[:, :128] + wide[:, 128:]
    u0[...] = first.reshape(4, 128, 128)
    high, low = split(first * (1.0 / TOKENS))
    u_pair[:, :128] = high
    u_pair[:, 128:] = low

    def hand_over(copies, buf, into):
        for p in range(4):
            place = at(x, p)
            target = device(place, y, x, owner)
            if p:
                copies.start(p, buf.at[place], into.at[slot], target, lands=slot)
            else:

                @pl.when(jnp.logical_not(stays))
                def _():
                    pltpu.make_async_remote_copy(
                        src_ref=buf.at[place], dst_ref=into.at[slot], send_sem=copies.send.at[0],
                        recv_sem=copies.recv.at[slot], device_id=target, device_id_type=MESH,
                    ).start()

                @pl.when(stays)
                def _():
                    pltpu.make_async_copy(buf.at[place], into.at[slot], copies.recv.at[slot]).start()

    def along(h, d):
        return heavy(1 - h, d)

    def multiply(h, s, d):
        lanes = slice(2 * s, 2 * s + 2)
        rows = x_full[0, at(x, d), lanes] if h == 0 else x_full[1, lanes, at(z, d)]
        wide = jnp.dot(rows.reshape(192, 512), u_pair[...], preferred_element_type=F32)
        value = (wide[:, :128] + wide[:, 128:]).reshape(2, 96, 128)
        if d == 0:
            v_own[h, s] = value
        else:
            keep(v_part.at[h, s, d - 1], value)
            vc.start(h * 6 + s * 3 + d - 1, v_part.at[h, s, d - 1], v_near.at[h, s, d - 1], along(h, d))

    for s in range(2):
        for d in (2, 1, 3):
            for h in range(2):
                multiply(h, s, d)
    keep(u_code, u0[...])
    hand_over(uc, u_code, u_in)
    for s in range(2):
        for h in range(2):
            multiply(h, s, 0)
    for s in range(2):
        for h in range(2):
            total = v_own[h, s]
            for d in (1, 3, 2):
                vc.arrived(h * 6 + s * 3 + d - 1, v_near.at[h, s, d - 1])
                total += decode(v_near.at[h, s, d - 1])
            keep(v_send.at[h, s], total)
            for d in (1, 3, 2):
                vc.start(12 + h * 6 + s * 3 + d - 1, v_send.at[h, s], v_line.at[h, s, d - 1], heavy(h, d))

    dots = []

    def use_v(h, s, d):
        along_place = at(x if h == 0 else z, -d)
        value = decode(v_code.at[h, along_place, 2 * s : 2 * s + 2])
        for k in range(2):
            lane = 2 * s + k
            place = along_place * 4 + lane if h == 0 else lane * 4 + along_place
            v_all[h, place] = value[k]
            dots.append(jnp.sum(value[k] * b_all[h, place], axis=0, keepdims=True))

    for s in range(2):
        for h in range(2):
            total = decode(v_send.at[h, s])
            for d in (1, 3, 2):
                vc.arrived(12 + h * 6 + s * 3 + d - 1, v_line.at[h, s, d - 1])
                total += decode(v_line.at[h, s, d - 1])
            mine_here = v_code.at[h, x if h == 0 else z, 2 * s : 2 * s + 2]
            keep(mine_here, total)
            for d in (1, 3, 2):
                vc.start(24 + h * 6 + s * 3 + d - 1, mine_here, mine_here, along(h, d))
            use_v(h, s, 0)
    for s in range(2):
        for h in range(2):
            for d in (1, 3, 2):
                vc.arrived(
                    24 + h * 6 + s * 3 + d - 1, v_code.at[h, at(x if h == 0 else z, -d), 2 * s : 2 * s + 2]
                )
                use_v(h, s, d)

    bv = sum(dots)
    alpha = bb / (bv + RIDGE * bb)
    norm = jnp.zeros((1, 128), F32)
    for h in range(2):
        value = b_all[h].reshape(1536, 128)
        residual = value - alpha * (v_all[h].reshape(1536, 128) + RIDGE * value)
        norm += jnp.sum(residual * residual, axis=0, keepdims=True)
        r_all[h] = residual
        high, low = split(residual)
        b_pair[h, :, :, :128] = high.reshape(16, 96, 128)
        b_pair[h, :, :, 128:] = low.reshape(16, 96, 128)
    beta = norm / bb
    wide = jnp.dot(x_flip[...], b_pair[...].reshape(TOKENS, 256), preferred_element_type=F32)
    turned = wide[:, :128] + wide[:, 128:] + beta * u0[...].reshape(512, 128)
    keep(d_code, turned.reshape(4, 128, 128))
    gamma[c, mine] = jnp.broadcast_to(jnp.sum(turned * turned, axis=0, keepdims=True), (8, 128))
    spread = [(dx, dz, e) for dx in (2, 1, 3, 0) for dz in (2, 1, 3, 0) for e in (0, 1) if dx or dz or e]
    for k, (dx, dz, e) in enumerate(spread):
        gc.start(k, gamma.at[c, mine], gamma.at[c, mine], device(at(x, dx), y, at(z, dz), lax.rem(c + e, 2)))
    hand_over(dc, d_code, d_in)
    dd = jnp.zeros((1, 128), F32)
    for h in range(2):
        turn = r_all[h] + beta * b_all[h].reshape(1536, 128)
        dd += jnp.sum(turn * turn, axis=0, keepdims=True)
    scalars[c, 0] = jnp.broadcast_to(alpha * (1.0 / TOKENS), (8, 128))
    scalars[c, 1] = jnp.broadcast_to(norm * (1.0 / TOKENS), (8, 128))
    scalars[c, 2] = jnp.broadcast_to(dd * RIDGE, (8, 128))
    tc.start(0, scalars.at[c], scalars.at[c], device(x, y, z, twin))
    tc.arrived(0, scalars.at[twin])
    for k, (dx, dz, e) in enumerate(spread):
        gc.arrived(k, gamma.at[lax.rem(c + e, 2), at(x, -dx) * 4 + at(z, -dz)])
    steps = []
    for e in range(2):
        curve = jnp.sum(gamma[e], axis=0)[:1] * (1.0 / TOKENS) + scalars[e, 2, :1]
        steps.append(scalars[e, 1, :1] / curve)
    for k in range(4):
        uc.arrived(k, u_in.at[k])
        dc.arrived(k, d_in.at[k])
    for k in range(4):
        t, e = k // 2, k % 2
        out_ref[t * 128 : t * 128 + 128, e * 128 : e * 128 + 128] = (
            scalars[e, 0, :1] * decode(u_in.at[k]) + steps[e] * decode(d_in.at[k])
        )

    @pl.when(jnp.logical_not(stays))
    def _():
        pltpu.make_async_copy(u_code.at[0], u_code.at[0], u_s.at[0]).wait()
        pltpu.make_async_copy(d_code.at[0], d_code.at[0], d_s.at[0]).wait()

    for copies in (wc, yc, xc, bc, vc, xyc, xcc, pc, gc, tc, uc, dc):
        copies.finish()


def local(activations, targets, key_weight):
    dma = pltpu.SemaphoreType.DMA
    buffers = [
        ((16, 96, 128), BF16),
        ((2, 96, 1024), BF16),
        ((4, 2, 96, 1024), BF16),
        ((2, 16, 128, 256), BF16),
        ((16, 96, 128), BF16),
        ((4, 2, 16, 96, 128), BF16),
        ((2, 4, 4, 96, 512), BF16),
        ((512, TOKENS), BF16),
        ((2, 192, 128), F32),
        ((192, 128), F32),
        ((2, 16, 112, 128), BF16),
        ((2, 16, 96, 128), F32),
        ((2, 16, 96, 256), BF16),
        ((4, 128, 128), F32),
        ((512, 256), BF16),
        ((4, 144, 128), BF16),
        ((4, 144, 128), BF16),
        ((2, 2, 2, 96, 128), F32),
        ((2, 2, 3, 2, 112, 128), BF16),
        ((2, 2, 3, 2, 112, 128), BF16),
        ((2, 2, 2, 112, 128), BF16),
        ((2, 2, 3, 2, 112, 128), BF16),
        ((2, 4, 4, 112, 128), BF16),
        ((2, 16, 96, 128), F32),
        ((2, 1536, 128), F32),
        ((2, 16, 8, 128), F32),
        ((2, 3, 8, 128), F32),
        ((4, 144, 128), BF16),
        ((4, 144, 128), BF16),
    ]
    counts = (7, 30, 15, 6, 4, 1, 30, 36, 31, 1, 4, 4)
    return pl.pallas_call(
        kernel,
        out_shape=jax.ShapeDtypeStruct((256, 256), F32),
        in_specs=[pl.BlockSpec(memory_space=pl.ANY)] * 3,
        out_specs=pl.BlockSpec(memory_space=pltpu.VMEM),
        scratch_shapes=[pltpu.VMEM(*b) for b in buffers] + [dma((34,))] + [dma((n,)) for n in counts for _ in range(2)],
        compiler_params=pltpu.CompilerParams(collective_id=0, has_side_effects=True, vmem_limit_bytes=56 * 2**20),
    )(activations, targets, key_weight)


def solution(mesh):
    placed = (P("dp", "tensor"), P("dp", "tensor"), P("dp", "tensor"))
    return jax.shard_map(local, mesh=mesh, in_specs=placed, out_specs=P("dp", "tensor"), check_vma=False)
```

```python
import jax
import jax.numpy as jnp
from jax import lax
from jax.experimental import pallas as pl
from jax.experimental.pallas import tpu as pltpu
from jax.sharding import PartitionSpec as P

MESH = pl.DeviceIdType.MESH
TOKENS = 3072
RIDGE = 0.5
F32, BF16 = jnp.float32, jnp.bfloat16


def device(x, y, z, c):
    return (x * 8 + z * 2 + c, y)


def split(value):
    high = value.astype(BF16)
    return high, (value - high.astype(F32)).astype(BF16)


def encode(value):
    top = jnp.max(jnp.abs(value), axis=-2, keepdims=True)
    scale = jnp.maximum(top * 1.03125, 1e-30).astype(BF16)
    inverse = 8.0 / scale.astype(F32)
    p = jnp.abs(value) * inverse + 0.125
    p = p * p
    p = p * p
    p8 = p * p
    p = p8 * p8
    p = p * p * p8
    code = jnp.where(value < 0, -p, p).astype(BF16)
    return code, jnp.broadcast_to(scale, scale.shape[:-2] + (16, 128))


def decode(ref):
    rows = ref.shape[-2] - 16
    code = ref[..., :rows, :].astype(F32)
    scale = ref[..., rows:, :].astype(F32)[..., :1, :] * 0.125
    p = jnp.exp2(jnp.log2(jnp.abs(code)) * (1.0 / 40.0))
    value = (p - 0.125) * scale
    return jnp.where(code < 0, -value, value)


def keep(ref, value):
    rows = value.shape[-2]
    ref[..., :rows, :], ref[..., rows:, :] = encode(value)


class Copies:
    def __init__(self, send, recv):
        self.send, self.recv, self.started = send, recv, []

    def start(self, index, src, dst, target, lands=None):
        copy = pltpu.make_async_remote_copy(
            src_ref=src,
            dst_ref=dst,
            send_sem=self.send.at[index],
            recv_sem=self.recv.at[index if lands is None else lands],
            device_id=target,
            device_id_type=MESH,
        )
        copy.start()
        self.started.append(copy)

    def arrived(self, index, dst):
        pltpu.make_async_copy(dst, dst, self.recv.at[index]).wait()

    def finish(self):
        for copy in self.started:
            copy.wait_send()


def kernel(
    x_in, y_in, w_in, out_ref,
    x_sort, y_sort, y_all, w_all, x_mine, x_all, x_full, x_flip,
    b_part, b_other, b_code, b_all, b_pair, u0, u_pair, u_code, d_code,
    v_own, v_part, v_near, v_send, v_line, v_code, v_all, r_all, gamma, scalars, u_in, d_in,
    l_s, y_s, y_r, w_s, w_r, x_s, x_r, xy_s, xy_r, xc_s, xc_r, p_s, p_r,
    b_s, b_r, v_s, v_r, g_s, g_r, t_s, t_r, u_s, u_r, d_s, d_r, line_sem, twin_sem,
):
    i = lax.axis_index("dp")
    y = lax.axis_index("tensor")
    x, z, c = i // 8, lax.rem(i // 2, 4), lax.rem(i, 2)
    mine = x * 4 + z
    twin = 1 - c

    def at(a, d):
        return lax.rem(a + d + 4, 4)

    partners = [(dx, dz) for dx in range(4) for dz in range(4) if dx or dz]
    up, down = at(y, 1), at(y, -1)

    slot = lax.rem(z, 2) * 2 + c
    owner = z // 2
    stays = jnp.logical_and(x == z, owner == c)
    barrier = pltpu.get_barrier_semaphore()
    peers = [device(at(x, d), y, z, c) for d in (1, 3, 2)] + [device(x, y, at(z, d), c) for d in (1, 3, 2)]
    peers += [device(x, place, z, e) for place in (up, down) for e in (c, twin)]
    peers += [device(x, y, z, twin)]
    for peer in peers:
        pl.semaphore_signal(barrier, inc=1, device_id=peer, device_id_type=MESH)

    loads = []
    for h in range(2):
        loads.append((w_in.at[h * 128 : h * 128 + 128, :], w_all.at[h, mine]))
    for e in range(2):
        for h in range(2):
            for q in range(4):
                columns = slice(q * 512 + e * 256 + h * 128, q * 512 + e * 256 + h * 128 + 128)
                loads.append((y_in.at[:, columns], y_sort.at[e, :, h * 512 + q * 128 : h * 512 + q * 128 + 128]))
    for k in range(16):
        loads.append((x_in.at[:, k * 128 : k * 128 + 128], x_sort.at[k]))
    loads = [pltpu.make_async_copy(src, dst, l_s.at[k]) for k, (src, dst) in enumerate(loads)]
    for load in loads:
        load.start()
    for load in loads:
        load.wait()
    pl.semaphore_wait(barrier, len(peers))
    for d in (1, 3, 2):
        pl.semaphore_signal(line_sem, inc=1, device_id=device(at(x, d), y, z, c), device_id_type=MESH)

    wc, yc, xc, xyc, xcc = Copies(w_s, w_r), Copies(y_s, y_r), Copies(x_s, x_r), Copies(xy_s, xy_r), Copies(xc_s, xc_r)
    pc, bc, vc = Copies(p_s, p_r), Copies(b_s, b_r), Copies(v_s, v_r)
    gc, tc, uc, dc = Copies(g_s, g_r), Copies(t_s, t_r), Copies(u_s, u_r), Copies(d_s, d_r)

    def light(h, d):
        return device(at(x, d), y, z, c) if h == 0 else device(x, y, at(z, d), c)

    def heavy(h, d):
        return device(x, y, at(z, d), c) if h == 0 else device(at(x, d), y, z, c)

    def block(h, dl, dh):
        return at(x, dl) * 4 + at(z, dh) if h == 0 else at(x, dh) * 4 + at(z, dl)

    def gather_first(copies, buf):
        for d in (1, 3, 2):
            for h in range(2):
                copies.start(h * 3 + d - 1, buf.at[h, mine], buf.at[h, mine], light(h, d))
        gather_heavy(copies, buf, 0)

    def gather_heavy(copies, buf, j):
        for h in range(2):
            part = buf.at[h, block(h, -j, 0)]
            if j:
                copies.arrived(h * 3 + j - 1, part)
            for d in (1, 3, 2):
                copies.start(6 + h * 12 + j * 3 + d - 1, part, part, heavy(h, d))

    def gather_rest(copies, buf, use):
        for j in (1, 3, 2):
            gather_heavy(copies, buf, j)
        for h in range(2):
            for j in (0, 1, 3, 2):
                use(h, block(h, -j, 0))

    def gather_last(copies, buf, use):
        for j in (0, 1, 3, 2):
            for h in range(2):
                for d in (1, 3, 2):
                    place = block(h, -j, -d)
                    copies.arrived(6 + h * 12 + j * 3 + d - 1, buf.at[h, place])
                    use(h, place)

    def ring_heavy(j):
        for h in range(2):
            part = w_all.at[h, block(h, -j, 0)]
            if j:
                wc.arrived(h * 3 + j - 1, part)
            wc.start(6 + h * 8 + j * 2, part, part, heavy(h, 1))
            wc.start(6 + h * 8 + j * 2 + 1, part, part, heavy(h, -1))

    def ring_forward(j):
        for h in range(2):
            k, d = (0, 1) if j in (0, 1) else (1, -1)
            part = w_all.at[h, block(h, -j, -d)]
            wc.arrived(6 + h * 8 + j * 2 + k, part)
            wc.start(22 + h * 4 + j, part, part, heavy(h, d))

    for flip in range(2):
        for e in range(2):
            target = lax.rem(c + e, 2)
            place = lax.rem(y + 1 + 2 * lax.rem(c + flip, 2), 4)
            yc.start(flip * 2 + e, y_sort.at[target], y_all.at[y, c], device(x, place, z, target), lands=flip * 2 + c)
    for d in (1, 3, 2):
        for h in range(2):
            wc.start(h * 3 + d - 1, w_all.at[h, mine], w_all.at[h, mine], light(h, d))
    ring_heavy(0)
    pl.semaphore_wait(line_sem, 3)
    for k, (dx, dz) in enumerate(partners):
        xc.start(k, x_sort.at[at(x, dx) * 4 + at(z, dz)], x_mine.at[mine], device(at(x, dx), y, at(z, dz), c))
    pl.semaphore_signal(twin_sem, inc=1, device_id=device(x, y, z, twin), device_id_type=MESH)
    yc.start(4, y_sort.at[twin], y_all.at[y, c], device(x, y, z, twin))
    y_all[y, c] = y_sort[c]
    x_mine[mine] = x_sort[mine]

    yc.arrived(0, y_all.at[down, 0])
    yc.start(5, y_all.at[down, 0], y_all.at[down, 0], device(x, up, z, c))
    yc.arrived(1, y_all.at[up, 1])
    yc.start(6, y_all.at[up, 1], y_all.at[up, 1], device(x, down, z, c))
    for k, (dx, dz) in enumerate(partners):
        xc.arrived(k, x_mine.at[at(x, -dx) * 4 + at(z, -dz)])

    def x_half(s, e, k):
        return x_all.at[s, e, k * 8 : k * 8 + 8]

    for flip in range(2):
        for k in range(2):
            place = up if k == flip else down
            xyc.start(flip * 2 + k, x_mine.at[k * 8 : k * 8 + 8], x_half(y, c, k), device(x, place, z, c))
    xcc.start(0, x_mine, x_all.at[y, c], device(x, y, z, twin))
    for j in (1, 3, 2):
        ring_heavy(j)
    x_all[y, c] = x_mine[...]
    for j in (0, 1, 3, 2):
        ring_forward(j)
    yc.arrived(2, y_all.at[up, 0])
    yc.arrived(3, y_all.at[down, 1])
    yc.arrived(4, y_all.at[y, twin])
    yc.arrived(5, y_all.at[at(y, 2), 0])
    yc.arrived(6, y_all.at[at(y, 2), 1])

    def product(j):
        for h in range(2):
            if j in (2, 3):
                wc.arrived(6 + h * 8 + j * 2, w_all.at[h, block(h, -j, -1)])
            else:
                wc.arrived(6 + h * 8 + j * 2 + 1, w_all.at[h, block(h, -j, 1)])
            wc.arrived(22 + h * 4 + j, w_all.at[h, block(h, -j, 2)])
        s = at(x, -j)
        total = jnp.dot(
            y_all[s, :, :, :512].reshape(192, 512),
            w_all[0, pl.ds(4 * s, 4)].reshape(512, 256),
            preferred_element_type=F32,
        )
        zz = at(z, -j)
        columns = pl.ds(pl.multiple_of(512 + zz * 128, 128), 128)
        for s in range(4):
            total += jnp.dot(
                y_all[s, :, :, columns].reshape(192, 128), w_all[1, s * 4 + zz], preferred_element_type=F32
            )
        return total

    part = product(0)
    part += product(1)
    xyc.arrived(0, x_half(down, c, 0))
    xyc.start(4, x_half(down, c, 0), x_half(down, c, 0), device(x, up, z, c))
    xyc.arrived(1, x_half(up, c, 1))
    xyc.start(5, x_half(up, c, 1), x_half(up, c, 1), device(x, down, z, c))
    part += product(3)
    part += product(2)
    b_part[0] = part[:, :128]
    b_part[1] = part[:, 128:]
    pc.start(0, b_part.at[twin], b_other, device(x, y, z, twin))
    pc.arrived(0, b_other)
    pl.semaphore_wait(twin_sem, 1)
    for h in range(2):
        keep(b_code.at[h, mine], b_part[c, h * 96 : h * 96 + 96] + b_other[h * 96 : h * 96 + 96])
    gather_first(bc, b_code)

    norms = []

    def use_b(h, place):
        value = decode(b_code.at[h, place])
        b_all[h, place] = value
        norms.append(jnp.sum(value * value, axis=0, keepdims=True))
        high, low = split(value)
        b_pair[h, place, :, :128] = high
        b_pair[h, place, :, 128:] = low

    gather_rest(bc, b_code, use_b)
    xyc.arrived(2, x_half(up, c, 0))
    xcc.start(3, x_all.at[up, c], x_all.at[up, c], device(x, y, z, twin))
    xyc.arrived(3, x_half(down, c, 1))
    xcc.start(1, x_all.at[down, c], x_all.at[down, c], device(x, y, z, twin))
    xyc.arrived(4, x_half(at(y, 2), c, 0))
    xyc.arrived(5, x_half(at(y, 2), c, 1))
    xcc.start(2, x_all.at[at(y, 2), c], x_all.at[at(y, 2), c], device(x, y, z, twin))

    def arrange(s, e):
        piece = x_all[s, e].reshape(1536, 128)
        columns = pl.ds(pl.multiple_of(s * 128, 128), 128)
        rows = pl.ds(pl.multiple_of(e * 1536, 128), 1536)
        x_full[e, :, :, :, columns] = piece.reshape(4, 4, 96, 128)
        x_flip[columns, rows] = piece.T

    for d in (0, 1, 3, 2):
        arrange(at(y, -d), c)
    for d in (0, 1, 3, 2):
        xcc.arrived(d, x_all.at[at(y, -d), twin])
        arrange(at(y, -d), twin)

    gather_last(bc, b_code, use_b)
    bb = sum(norms)
    wide = jnp.dot(x_flip[...], b_pair[...].reshape(TOKENS, 256), preferred_element_type=F32)
    first = wide[:, :128] + wide[:, 128:]
    u0[...] = first.reshape(4, 128, 128)
    high, low = split(first * (1.0 / TOKENS))
    u_pair[:, :128] = high
    u_pair[:, 128:] = low

    def hand_over(copies, buf, into):
        for p in range(4):
            place = at(x, p)
            target = device(place, y, x, owner)
            if p:
                copies.start(p, buf.at[place], into.at[slot], target, lands=slot)
            else:

                @pl.when(jnp.logical_not(stays))
                def _():
                    pltpu.make_async_remote_copy(
                        src_ref=buf.at[place], dst_ref=into.at[slot], send_sem=copies.send.at[0],
                        recv_sem=copies.recv.at[slot], device_id=target, device_id_type=MESH,
                    ).start()

                @pl.when(stays)
                def _():
                    pltpu.make_async_copy(buf.at[place], into.at[slot], copies.recv.at[slot]).start()

    def along(h, d):
        return heavy(1 - h, d)

    def multiply(h, s, d):
        lanes = slice(2 * s, 2 * s + 2)
        rows = x_full[0, at(x, d), lanes] if h == 0 else x_full[1, lanes, at(z, d)]
        wide = jnp.dot(rows.reshape(192, 512), u_pair[...], preferred_element_type=F32)
        value = wide[:, :128] + wide[:, 128:]
        if d == 0:
            v_own[h, s] = value
        else:
            keep(v_part.at[h, s, d - 1], value)
            vc.start(h * 6 + s * 3 + d - 1, v_part.at[h, s, d - 1], v_near.at[h, s, d - 1], along(h, d))

    for s in range(2):
        for d in (2, 1, 3):
            for h in range(2):
                multiply(h, s, d)
    keep(u_code, u0[...])
    hand_over(uc, u_code, u_in)
    for s in range(2):
        for h in range(2):
            multiply(h, s, 0)
    for s in range(2):
        for h in range(2):
            total = v_own[h, s]
            for d in (1, 3, 2):
                vc.arrived(h * 6 + s * 3 + d - 1, v_near.at[h, s, d - 1])
                total += decode(v_near.at[h, s, d - 1])
            keep(v_send.at[h, s], total)
            for d in (1, 3, 2):
                vc.start(12 + h * 6 + s * 3 + d - 1, v_send.at[h, s], v_line.at[h, s, d - 1], heavy(h, d))

    dots = []

    def use_v(h, s, d):
        along_place = at(x if h == 0 else z, -d)
        value = decode(v_code.at[h, along_place, s]).reshape(2, 96, 128)
        for k in range(2):
            lane = 2 * s + k
            place = along_place * 4 + lane if h == 0 else lane * 4 + along_place
            v_all[h, place] = value[k]
            dots.append(jnp.sum(value[k] * b_all[h, place], axis=0, keepdims=True))

    for s in range(2):
        for h in range(2):
            total = decode(v_send.at[h, s])
            for d in (1, 3, 2):
                vc.arrived(12 + h * 6 + s * 3 + d - 1, v_line.at[h, s, d - 1])
                total += decode(v_line.at[h, s, d - 1])
            mine_here = v_code.at[h, x if h == 0 else z, s]
            keep(mine_here, total)
            for d in (1, 3, 2):
                vc.start(24 + h * 6 + s * 3 + d - 1, mine_here, mine_here, along(h, d))
            use_v(h, s, 0)
    for s in range(2):
        for h in range(2):
            for d in (1, 3, 2):
                vc.arrived(24 + h * 6 + s * 3 + d - 1, v_code.at[h, at(x if h == 0 else z, -d), s])
                use_v(h, s, d)

    bv = sum(dots)
    alpha = bb / (bv + RIDGE * bb)
    norm = jnp.zeros((1, 128), F32)
    for h in range(2):
        value = b_all[h].reshape(1536, 128)
        residual = value - alpha * (v_all[h].reshape(1536, 128) + RIDGE * value)
        norm += jnp.sum(residual * residual, axis=0, keepdims=True)
        r_all[h] = residual
        high, low = split(residual)
        b_pair[h, :, :, :128] = high.reshape(16, 96, 128)
        b_pair[h, :, :, 128:] = low.reshape(16, 96, 128)
    beta = norm / bb
    wide = jnp.dot(x_flip[...], b_pair[...].reshape(TOKENS, 256), preferred_element_type=F32)
    turned = wide[:, :128] + wide[:, 128:] + beta * u0[...].reshape(512, 128)
    gamma[c, mine] = jnp.broadcast_to(jnp.sum(turned * turned, axis=0, keepdims=True), (8, 128))
    spread = [(dx, dz, e) for dx in (2, 1, 3, 0) for dz in (2, 1, 3, 0) for e in (0, 1) if dx or dz or e]
    for k, (dx, dz, e) in enumerate(spread):
        gc.start(k, gamma.at[c, mine], gamma.at[c, mine], device(at(x, dx), y, at(z, dz), lax.rem(c + e, 2)))
    keep(d_code, turned.reshape(4, 128, 128))
    hand_over(dc, d_code, d_in)
    dd = jnp.zeros((1, 128), F32)
    for h in range(2):
        turn = r_all[h] + beta * b_all[h].reshape(1536, 128)
        dd += jnp.sum(turn * turn, axis=0, keepdims=True)
    scalars[c, 0] = jnp.broadcast_to(alpha * (1.0 / TOKENS), (8, 128))
    scalars[c, 1] = jnp.broadcast_to(norm * (1.0 / TOKENS), (8, 128))
    scalars[c, 2] = jnp.broadcast_to(dd * RIDGE, (8, 128))
    tc.start(0, scalars.at[c], scalars.at[c], device(x, y, z, twin))
    tc.arrived(0, scalars.at[twin])
    for k, (dx, dz, e) in enumerate(spread):
        gc.arrived(k, gamma.at[lax.rem(c + e, 2), at(x, -dx) * 4 + at(z, -dz)])
    steps = []
    for e in range(2):
        curve = jnp.sum(gamma[e], axis=0)[:1] * (1.0 / TOKENS) + scalars[e, 2, :1]
        steps.append(scalars[e, 1, :1] / curve)
    for k in range(4):
        uc.arrived(k, u_in.at[k])
        dc.arrived(k, d_in.at[k])
    for k in range(4):
        t, e = k // 2, k % 2
        out_ref[t * 128 : t * 128 + 128, e * 128 : e * 128 + 128] = (
            scalars[e, 0, :1] * decode(u_in.at[k]) + steps[e] * decode(d_in.at[k])
        )

    @pl.when(jnp.logical_not(stays))
    def _():
        pltpu.make_async_copy(u_code.at[0], u_code.at[0], u_s.at[0]).wait()
        pltpu.make_async_copy(d_code.at[0], d_code.at[0], d_s.at[0]).wait()

    for copies in (wc, yc, xc, bc, vc, xyc, xcc, pc, gc, tc, uc, dc):
        copies.finish()


def local(activations, targets, key_weight):
    dma = pltpu.SemaphoreType.DMA
    buffers = [
        ((16, 96, 128), BF16),
        ((2, 96, 1024), BF16),
        ((4, 2, 96, 1024), BF16),
        ((2, 16, 128, 256), BF16),
        ((16, 96, 128), BF16),
        ((4, 2, 16, 96, 128), BF16),
        ((2, 4, 4, 96, 512), BF16),
        ((512, TOKENS), BF16),
        ((2, 192, 128), F32),
        ((192, 128), F32),
        ((2, 16, 112, 128), BF16),
        ((2, 16, 96, 128), F32),
        ((2, 16, 96, 256), BF16),
        ((4, 128, 128), F32),
        ((512, 256), BF16),
        ((4, 144, 128), BF16),
        ((4, 144, 128), BF16),
        ((2, 2, 192, 128), F32),
        ((2, 2, 3, 208, 128), BF16),
        ((2, 2, 3, 208, 128), BF16),
        ((2, 2, 208, 128), BF16),
        ((2, 2, 3, 208, 128), BF16),
        ((2, 4, 2, 208, 128), BF16),
        ((2, 16, 96, 128), F32),
        ((2, 1536, 128), F32),
        ((2, 16, 8, 128), F32),
        ((2, 3, 8, 128), F32),
        ((4, 144, 128), BF16),
        ((4, 144, 128), BF16),
    ]
    counts = (7, 30, 15, 6, 4, 1, 30, 36, 31, 1, 4, 4)
    return pl.pallas_call(
        kernel,
        out_shape=jax.ShapeDtypeStruct((256, 256), F32),
        in_specs=[pl.BlockSpec(memory_space=pl.ANY)] * 3,
        out_specs=pl.BlockSpec(memory_space=pltpu.VMEM),
        scratch_shapes=[pltpu.VMEM(*b) for b in buffers] + [dma((34,))] + [dma((n,)) for n in counts for _ in range(2)]
        + [pltpu.SemaphoreType.REGULAR] * 2,
        compiler_params=pltpu.CompilerParams(collective_id=0, has_side_effects=True, vmem_limit_bytes=56 * 2**20),
    )(activations, targets, key_weight)


def solution(mesh):
    placed = (P("dp", "tensor"), P("dp", "tensor"), P("dp", "tensor"))
    return jax.shard_map(local, mesh=mesh, in_specs=placed, out_specs=P("dp", "tensor"), check_vma=False)
```

```python
import jax
import jax.numpy as jnp
from jax import lax
from jax.experimental import pallas as pl
from jax.experimental.pallas import tpu as pltpu
from jax.sharding import PartitionSpec as P

MESH = pl.DeviceIdType.MESH
TOKENS = 3072
RIDGE = 0.5
F32, BF16 = jnp.float32, jnp.bfloat16


def device(x, y, z, c):
    return (x * 8 + z * 2 + c, y)


def split(value):
    high = value.astype(BF16)
    return high, (value - high.astype(F32)).astype(BF16)


def encode(value):
    top = jnp.max(jnp.abs(value), axis=-2, keepdims=True)
    scale = jnp.maximum(top * 1.03125, 1e-30).astype(BF16)
    inverse = 8.0 / scale.astype(F32)
    p = jnp.abs(value) * inverse + 0.125
    p = p * p
    p = p * p
    p8 = p * p
    p = p8 * p8
    p = p * p * p8
    code = jnp.where(value < 0, -p, p).astype(BF16)
    return code, jnp.broadcast_to(scale, scale.shape[:-2] + (16, 128))


def decode(ref):
    rows = ref.shape[-2] - 16
    code = ref[..., :rows, :].astype(F32)
    scale = ref[..., rows:, :].astype(F32)[..., :1, :] * 0.125
    p = jnp.exp2(jnp.log2(jnp.abs(code)) * (1.0 / 40.0))
    value = (p - 0.125) * scale
    return jnp.where(code < 0, -value, value)


def keep(ref, value):
    rows = value.shape[-2]
    ref[..., :rows, :], ref[..., rows:, :] = encode(value)


class Copies:
    def __init__(self, send, recv):
        self.send, self.recv, self.started = send, recv, []

    def start(self, index, src, dst, target, lands=None):
        copy = pltpu.make_async_remote_copy(
            src_ref=src,
            dst_ref=dst,
            send_sem=self.send.at[index],
            recv_sem=self.recv.at[index if lands is None else lands],
            device_id=target,
            device_id_type=MESH,
        )
        copy.start()
        self.started.append(copy)

    def arrived(self, index, dst):
        pltpu.make_async_copy(dst, dst, self.recv.at[index]).wait()

    def finish(self):
        for copy in self.started:
            copy.wait_send()


def kernel(
    x_in, y_in, w_in, out_ref,
    x_sort, y_sort, y_all, w_all, x_mine, x_all, x_full, x_flip,
    b_part, b_other, b_code, b_all, b_pair, u0, u_pair, u_code, d_code,
    v_own, v_part, v_near, v_send, v_line, v_code, v_all, r_all, gamma, scalars, u_in, d_in,
    l_s, y_s, y_r, w_s, w_r, x_s, x_r, xy_s, xy_r, xc_s, xc_r, p_s, p_r,
    b_s, b_r, v_s, v_r, g_s, g_r, t_s, t_r, u_s, u_r, d_s, d_r, line_sem, twin_sem,
):
    i = lax.axis_index("dp")
    y = lax.axis_index("tensor")
    x, z, c = i // 8, lax.rem(i // 2, 4), lax.rem(i, 2)
    mine = x * 4 + z
    twin = 1 - c

    def at(a, d):
        return lax.rem(a + d + 4, 4)

    partners = [(dx, dz) for dx in range(4) for dz in range(4) if dx or dz]
    up, down = at(y, 1), at(y, -1)

    slot = lax.rem(z, 2) * 2 + c
    owner = z // 2
    stays = jnp.logical_and(x == z, owner == c)
    barrier = pltpu.get_barrier_semaphore()
    peers = [device(at(x, d), y, z, c) for d in (1, 3, 2)] + [device(x, y, at(z, d), c) for d in (1, 3, 2)]
    peers += [device(x, place, z, e) for place in (up, down) for e in (c, twin)]
    peers += [device(x, y, z, twin)]
    for peer in peers:
        pl.semaphore_signal(barrier, inc=1, device_id=peer, device_id_type=MESH)

    loads = []
    for h in range(2):
        loads.append((w_in.at[h * 128 : h * 128 + 128, :], w_all.at[h, mine]))
    for e in range(2):
        for h in range(2):
            for q in range(4):
                columns = slice(q * 512 + e * 256 + h * 128, q * 512 + e * 256 + h * 128 + 128)
                loads.append((y_in.at[:, columns], y_sort.at[e, :, h * 512 + q * 128 : h * 512 + q * 128 + 128]))
    for k in range(16):
        loads.append((x_in.at[:, k * 128 : k * 128 + 128], x_sort.at[k]))
    loads = [pltpu.make_async_copy(src, dst, l_s.at[k]) for k, (src, dst) in enumerate(loads)]
    for load in loads:
        load.start()
    for load in loads:
        load.wait()
    pl.semaphore_wait(barrier, len(peers))
    for d in (1, 3, 2):
        pl.semaphore_signal(line_sem, inc=1, device_id=device(at(x, d), y, z, c), device_id_type=MESH)

    wc, yc, xc, xyc, xcc = Copies(w_s, w_r), Copies(y_s, y_r), Copies(x_s, x_r), Copies(xy_s, xy_r), Copies(xc_s, xc_r)
    pc, bc, vc = Copies(p_s, p_r), Copies(b_s, b_r), Copies(v_s, v_r)
    gc, tc, uc, dc = Copies(g_s, g_r), Copies(t_s, t_r), Copies(u_s, u_r), Copies(d_s, d_r)

    def light(h, d):
        return device(at(x, d), y, z, c) if h == 0 else device(x, y, at(z, d), c)

    def heavy(h, d):
        return device(x, y, at(z, d), c) if h == 0 else device(at(x, d), y, z, c)

    def block(h, dl, dh):
        return at(x, dl) * 4 + at(z, dh) if h == 0 else at(x, dh) * 4 + at(z, dl)

    def gather_first(copies, buf):
        for d in (1, 3, 2):
            for h in range(2):
                copies.start(h * 3 + d - 1, buf.at[h, mine], buf.at[h, mine], light(h, d))
        gather_heavy(copies, buf, 0)

    def gather_heavy(copies, buf, j):
        for h in range(2):
            part = buf.at[h, block(h, -j, 0)]
            if j:
                copies.arrived(h * 3 + j - 1, part)
            for d in (1, 3, 2):
                copies.start(6 + h * 12 + j * 3 + d - 1, part, part, heavy(h, d))

    def gather_rest(copies, buf, use):
        for j in (1, 3, 2):
            gather_heavy(copies, buf, j)
        for h in range(2):
            for j in (0, 1, 3, 2):
                use(h, j, 0)

    def gather_last(copies, buf, use, done):
        for j in (0, 1, 3, 2):
            for h in range(2):
                for d in (1, 3, 2):
                    copies.arrived(6 + h * 12 + j * 3 + d - 1, buf.at[h, block(h, -j, -d)])
                    use(h, j, d)
                done(h, j)

    def ring_heavy(j):
        for h in range(2):
            part = w_all.at[h, block(h, -j, 0)]
            if j:
                wc.arrived(h * 3 + j - 1, part)
            wc.start(6 + h * 8 + j * 2, part, part, heavy(h, 1))
            wc.start(6 + h * 8 + j * 2 + 1, part, part, heavy(h, -1))

    def ring_forward(j):
        for h in range(2):
            k, d = (0, 1) if j in (0, 1) else (1, -1)
            part = w_all.at[h, block(h, -j, -d)]
            wc.arrived(6 + h * 8 + j * 2 + k, part)
            wc.start(22 + h * 4 + j, part, part, heavy(h, d))

    for flip in range(2):
        for e in range(2):
            target = lax.rem(c + e, 2)
            place = lax.rem(y + 1 + 2 * lax.rem(c + flip, 2), 4)
            yc.start(flip * 2 + e, y_sort.at[target], y_all.at[y, c], device(x, place, z, target), lands=flip * 2 + c)
    for d in (1, 3, 2):
        for h in range(2):
            wc.start(h * 3 + d - 1, w_all.at[h, mine], w_all.at[h, mine], light(h, d))
    ring_heavy(0)
    pl.semaphore_wait(line_sem, 3)
    for k, (dx, dz) in enumerate(partners):
        xc.start(k, x_sort.at[at(x, dx) * 4 + at(z, dz)], x_mine.at[mine], device(at(x, dx), y, at(z, dz), c))
    pl.semaphore_signal(twin_sem, inc=1, device_id=device(x, y, z, twin), device_id_type=MESH)
    yc.start(4, y_sort.at[twin], y_all.at[y, c], device(x, y, z, twin))
    y_all[y, c] = y_sort[c]
    x_mine[mine] = x_sort[mine]

    yc.arrived(0, y_all.at[down, 0])
    yc.start(5, y_all.at[down, 0], y_all.at[down, 0], device(x, up, z, c))
    yc.arrived(1, y_all.at[up, 1])
    yc.start(6, y_all.at[up, 1], y_all.at[up, 1], device(x, down, z, c))
    for k, (dx, dz) in enumerate(partners):
        xc.arrived(k, x_mine.at[at(x, -dx) * 4 + at(z, -dz)])

    def x_half(s, e, k):
        return x_all.at[s, e, k * 8 : k * 8 + 8]

    for flip in range(2):
        for k in range(2):
            place = up if k == flip else down
            xyc.start(flip * 2 + k, x_mine.at[k * 8 : k * 8 + 8], x_half(y, c, k), device(x, place, z, c))
    xcc.start(0, x_mine, x_all.at[y, c], device(x, y, z, twin))
    for j in (1, 3, 2):
        ring_heavy(j)
    x_all[y, c] = x_mine[...]
    for j in (0, 1, 3, 2):
        ring_forward(j)
    yc.arrived(2, y_all.at[up, 0])
    yc.arrived(3, y_all.at[down, 1])
    yc.arrived(4, y_all.at[y, twin])
    yc.arrived(5, y_all.at[at(y, 2), 0])
    yc.arrived(6, y_all.at[at(y, 2), 1])

    def product(j):
        for h in range(2):
            if j in (2, 3):
                wc.arrived(6 + h * 8 + j * 2, w_all.at[h, block(h, -j, -1)])
            else:
                wc.arrived(6 + h * 8 + j * 2 + 1, w_all.at[h, block(h, -j, 1)])
            wc.arrived(22 + h * 4 + j, w_all.at[h, block(h, -j, 2)])
        s = at(x, -j)
        total = jnp.dot(
            y_all[s, :, :, :512].reshape(192, 512),
            w_all[0, pl.ds(4 * s, 4)].reshape(512, 256),
            preferred_element_type=F32,
        )
        zz = at(z, -j)
        columns = pl.ds(pl.multiple_of(512 + zz * 128, 128), 128)
        for s in range(4):
            total += jnp.dot(
                y_all[s, :, :, columns].reshape(192, 128), w_all[1, s * 4 + zz], preferred_element_type=F32
            )
        return total

    part = product(0)
    part += product(1)
    xyc.arrived(0, x_half(down, c, 0))
    xyc.start(4, x_half(down, c, 0), x_half(down, c, 0), device(x, up, z, c))
    xyc.arrived(1, x_half(up, c, 1))
    xyc.start(5, x_half(up, c, 1), x_half(up, c, 1), device(x, down, z, c))
    part += product(3)
    part += product(2)
    b_part[0] = part[:, :128]
    b_part[1] = part[:, 128:]
    for h in range(2):
        rows = slice(h * 96, h * 96 + 96)
        pc.start(h, b_part.at[twin, rows], b_other.at[rows], device(x, y, z, twin))
    pl.semaphore_wait(twin_sem, 1)
    for h in range(2):
        pc.arrived(h, b_other.at[h * 96 : h * 96 + 96])
        keep(b_code.at[h, mine], b_part[c, h * 96 : h * 96 + 96] + b_other[h * 96 : h * 96 + 96])
    gather_first(bc, b_code)

    norms = []

    first_axis, second_axis = (x, z), (z, x)
    wide = [jnp.zeros((512, 256), F32)]

    def accumulate(h, j):
        group = at(first_axis[h], -j)
        tokens = pl.ds(pl.multiple_of(h * 1536 + group * 384, 128), 384)
        wide[0] += jnp.dot(
            x_flip[:, tokens], b_pair[h, pl.ds(group * 4, 4)].reshape(384, 256), preferred_element_type=F32
        )

    def use_b(h, j, d):
        place = at(first_axis[h], -j) * 4 + at(second_axis[h], -d)
        value = decode(b_code.at[h, block(h, -j, -d)])
        b_all[h, place] = value
        norms.append(jnp.sum(value * value, axis=0, keepdims=True))
        high, low = split(value)
        b_pair[h, place, :, :128] = high
        b_pair[h, place, :, 128:] = low

    def arrange(s, e):
        piece = x_all[s, e].reshape(1536, 128)
        columns = pl.ds(pl.multiple_of(s * 128, 128), 128)
        x_full[e, :, :, :, columns] = piece.reshape(4, 4, 96, 128)
        for m in range(4):
            group = [x_all[s, e, m * 4 + k + 3 * e * (k - m)] for k in range(4)]
            tokens = pl.ds(pl.multiple_of(e * 1536 + m * 384, 128), 384)
            x_flip[columns, tokens] = jnp.concatenate(group, axis=0).T

    xyc.arrived(2, x_half(up, c, 0))
    xcc.start(3, x_all.at[up, c], x_all.at[up, c], device(x, y, z, twin))
    xyc.arrived(3, x_half(down, c, 1))
    xcc.start(1, x_all.at[down, c], x_all.at[down, c], device(x, y, z, twin))
    for s in (y, up, down):
        arrange(s, c)
    gather_rest(bc, b_code, use_b)
    xyc.arrived(4, x_half(at(y, 2), c, 0))
    xyc.arrived(5, x_half(at(y, 2), c, 1))
    xcc.start(2, x_all.at[at(y, 2), c], x_all.at[at(y, 2), c], device(x, y, z, twin))
    arrange(at(y, 2), c)
    for d in (0, 3, 1, 2):
        xcc.arrived(d, x_all.at[at(y, -d), twin])
        arrange(at(y, -d), twin)

    gather_last(bc, b_code, use_b, accumulate)
    bb = sum(norms)
    first = wide[0][:, :128] + wide[0][:, 128:]
    wide[0] = jnp.zeros((512, 256), F32)
    u0[...] = first.reshape(4, 128, 128)
    high, low = split(first * (1.0 / TOKENS))
    u_pair[:, :128] = high
    u_pair[:, 128:] = low

    def hand_over(copies, buf, into):
        for p in range(4):
            place = at(x, p)
            target = device(place, y, x, owner)
            if p:
                copies.start(p, buf.at[place], into.at[slot], target, lands=slot)
            else:

                @pl.when(jnp.logical_not(stays))
                def _():
                    pltpu.make_async_remote_copy(
                        src_ref=buf.at[place], dst_ref=into.at[slot], send_sem=copies.send.at[0],
                        recv_sem=copies.recv.at[slot], device_id=target, device_id_type=MESH,
                    ).start()

                @pl.when(stays)
                def _():
                    pltpu.make_async_copy(buf.at[place], into.at[slot], copies.recv.at[slot]).start()

    def along(h, d):
        return heavy(1 - h, d)

    def multiply(h, s, d):
        lanes = slice(2 * s, 2 * s + 2)
        rows = x_full[0, at(x, d), lanes] if h == 0 else x_full[1, lanes, at(z, d)]
        both = jnp.dot(rows.reshape(192, 512), u_pair[...], preferred_element_type=F32)
        value = both[:, :128] + both[:, 128:]
        if d == 0:
            v_own[h, s] = value
        else:
            keep(v_part.at[h, s, d - 1], value)
            vc.start(h * 6 + s * 3 + d - 1, v_part.at[h, s, d - 1], v_near.at[h, s, d - 1], along(h, d))

    for s in range(2):
        for d in (2, 1, 3):
            for h in range(2):
                multiply(h, s, d)
    keep(u_code, u0[...])
    hand_over(uc, u_code, u_in)
    for s in range(2):
        for h in range(2):
            multiply(h, s, 0)
    for s in range(2):
        for h in range(2):
            total = v_own[h, s]
            for d in (1, 3, 2):
                vc.arrived(h * 6 + s * 3 + d - 1, v_near.at[h, s, d - 1])
                total += decode(v_near.at[h, s, d - 1])
            keep(v_send.at[h, s], total)
            for d in (1, 3, 2):
                vc.start(12 + h * 6 + s * 3 + d - 1, v_send.at[h, s], v_line.at[h, s, d - 1], heavy(h, d))

    dots = []

    def use_v(h, s, d):
        along_place = at(x if h == 0 else z, -d)
        value = decode(v_code.at[h, along_place, s]).reshape(2, 96, 128)
        for k in range(2):
            place = along_place * 4 + 2 * s + k
            v_all[h, place] = value[k]
            dots.append(jnp.sum(value[k] * b_all[h, place], axis=0, keepdims=True))
            high, low = split(value[k])
            b_pair[h, place, :, :128] = high
            b_pair[h, place, :, 128:] = low
        if s == 1:
            accumulate(h, d)

    for s in range(2):
        for h in range(2):
            total = decode(v_send.at[h, s])
            for d in (1, 3, 2):
                vc.arrived(12 + h * 6 + s * 3 + d - 1, v_line.at[h, s, d - 1])
                total += decode(v_line.at[h, s, d - 1])
            mine_here = v_code.at[h, x if h == 0 else z, s]
            keep(mine_here, total)
            for d in (1, 3, 2):
                vc.start(24 + h * 6 + s * 3 + d - 1, mine_here, mine_here, along(h, d))
            use_v(h, s, 0)
    for s in range(2):
        for h in range(2):
            for d in (1, 3, 2):
                vc.arrived(24 + h * 6 + s * 3 + d - 1, v_code.at[h, at(x if h == 0 else z, -d), s])
                use_v(h, s, d)

    bv = sum(dots)
    alpha = bb / (bv + RIDGE * bb)
    norm = jnp.zeros((1, 128), F32)
    for h in range(2):
        value = b_all[h].reshape(1536, 128)
        residual = value - alpha * (v_all[h].reshape(1536, 128) + RIDGE * value)
        norm += jnp.sum(residual * residual, axis=0, keepdims=True)
        r_all[h] = residual
    beta = norm / bb
    turned = (1.0 - RIDGE * alpha + beta) * u0[...].reshape(512, 128) - alpha * (wide[0][:, :128] + wide[0][:, 128:])
    gamma[c, mine] = jnp.broadcast_to(jnp.sum(turned * turned, axis=0, keepdims=True), (8, 128))
    spread = [(dx, dz, e) for dx in (2, 1, 3, 0) for dz in (2, 1, 3, 0) for e in (0, 1) if dx or dz or e]
    for k, (dx, dz, e) in enumerate(spread):
        gc.start(k, gamma.at[c, mine], gamma.at[c, mine], device(at(x, dx), y, at(z, dz), lax.rem(c + e, 2)))
    keep(d_code, turned.reshape(4, 128, 128))
    hand_over(dc, d_code, d_in)
    dd = jnp.zeros((1, 128), F32)
    for h in range(2):
        turn = r_all[h] + beta * b_all[h].reshape(1536, 128)
        dd += jnp.sum(turn * turn, axis=0, keepdims=True)
    scalars[c, 0] = jnp.broadcast_to(alpha * (1.0 / TOKENS), (8, 128))
    scalars[c, 1] = jnp.broadcast_to(norm * (1.0 / TOKENS), (8, 128))
    scalars[c, 2] = jnp.broadcast_to(dd * RIDGE, (8, 128))
    tc.start(0, scalars.at[c], scalars.at[c], device(x, y, z, twin))
    tc.arrived(0, scalars.at[twin])
    for k, (dx, dz, e) in enumerate(spread):
        gc.arrived(k, gamma.at[lax.rem(c + e, 2), at(x, -dx) * 4 + at(z, -dz)])
    steps = []
    for e in range(2):
        curve = jnp.sum(gamma[e], axis=0)[:1] * (1.0 / TOKENS) + scalars[e, 2, :1]
        steps.append(scalars[e, 1, :1] / curve)
    for k in range(4):
        uc.arrived(k, u_in.at[k])
        dc.arrived(k, d_in.at[k])
    for k in range(4):
        t, e = k // 2, k % 2
        out_ref[t * 128 : t * 128 + 128, e * 128 : e * 128 + 128] = (
            scalars[e, 0, :1] * decode(u_in.at[k]) + steps[e] * decode(d_in.at[k])
        )

    @pl.when(jnp.logical_not(stays))
    def _():
        pltpu.make_async_copy(u_code.at[0], u_code.at[0], u_s.at[0]).wait()
        pltpu.make_async_copy(d_code.at[0], d_code.at[0], d_s.at[0]).wait()

    for copies in (wc, yc, xc, bc, vc, xyc, xcc, pc, gc, tc, uc, dc):
        copies.finish()


def local(activations, targets, key_weight):
    dma = pltpu.SemaphoreType.DMA
    buffers = [
        ((16, 96, 128), BF16),
        ((2, 96, 1024), BF16),
        ((4, 2, 96, 1024), BF16),
        ((2, 16, 128, 256), BF16),
        ((16, 96, 128), BF16),
        ((4, 2, 16, 96, 128), BF16),
        ((2, 4, 4, 96, 512), BF16),
        ((512, TOKENS), BF16),
        ((2, 192, 128), F32),
        ((192, 128), F32),
        ((2, 16, 112, 128), BF16),
        ((2, 16, 96, 128), F32),
        ((2, 16, 96, 256), BF16),
        ((4, 128, 128), F32),
        ((512, 256), BF16),
        ((4, 144, 128), BF16),
        ((4, 144, 128), BF16),
        ((2, 2, 192, 128), F32),
        ((2, 2, 3, 208, 128), BF16),
        ((2, 2, 3, 208, 128), BF16),
        ((2, 2, 208, 128), BF16),
        ((2, 2, 3, 208, 128), BF16),
        ((2, 4, 2, 208, 128), BF16),
        ((2, 16, 96, 128), F32),
        ((2, 1536, 128), F32),
        ((2, 16, 8, 128), F32),
        ((2, 3, 8, 128), F32),
        ((4, 144, 128), BF16),
        ((4, 144, 128), BF16),
    ]
    counts = (7, 30, 15, 6, 4, 2, 30, 36, 31, 1, 4, 4)
    return pl.pallas_call(
        kernel,
        out_shape=jax.ShapeDtypeStruct((256, 256), F32),
        in_specs=[pl.BlockSpec(memory_space=pl.ANY)] * 3,
        out_specs=pl.BlockSpec(memory_space=pltpu.VMEM),
        scratch_shapes=[pltpu.VMEM(*b) for b in buffers] + [dma((34,))] + [dma((n,)) for n in counts for _ in range(2)]
        + [pltpu.SemaphoreType.REGULAR] * 2,
        compiler_params=pltpu.CompilerParams(collective_id=0, has_side_effects=True, vmem_limit_bytes=56 * 2**20),
    )(activations, targets, key_weight)


def solution(mesh):
    placed = (P("dp", "tensor"), P("dp", "tensor"), P("dp", "tensor"))
    return jax.shard_map(local, mesh=mesh, in_specs=placed, out_specs=P("dp", "tensor"), check_vma=False)
```
